128 devices in a mesh: dp: 16 (over x, z_hi, core), tensor: 8 (over z_lo, y).
Axes of the slice: x: 4, y: 4, z: 4 (z_hi: 2, z_lo: 2; z = z_hi * 2 + z_lo), core: 2. Of those that a mesh axis runs over, the one named last changes fastest.
Arguments:
- residual: bfloat16 [2048, 2880], P('dp'), may hold values from -6 to 6
- attn_gain: bfloat16 [2880], P('dp'), may hold values from 0.5 to 1.5
- query_weight: bfloat16 [2880, 4096], P('dp', 'tensor'), may hold values from -0.109375 to 0.109375
- query_bias: bfloat16 [4096], P('tensor'), may hold values from -0.59765625 to 0.59765625
- key_matrix: bfloat16 [2880, 512], P('dp', 'tensor'), may hold values from -0.109375 to 0.109375
- key_offset_bias: bfloat16 [512], P('tensor'), may hold values from -0.59765625 to 0.59765625
- value_matrix: bfloat16 [2880, 512], P('dp', 'tensor'), may hold values from -0.109375 to 0.109375
- value_offset_bias: bfloat16 [512], P('tensor'), may hold values from -0.59765625 to 0.59765625
- attention_sink_logits: bfloat16 [64], P('tensor'), may hold values from -3 to 3
- out_weight: bfloat16 [2880, 4096], P('dp', 'tensor'), may hold values from -1 to 1
- out_bias: bfloat16 [2880], P('dp'), may hold values from -0.59765625 to 0.59765625
- mlp_gain: bfloat16 [2880], P('dp'), may hold values from 0.5 to 1.5
- router_weight: bfloat16 [2880, 16], P('dp'), may hold values from -0.0546875 to 0.0546875
- router_bias: bfloat16 [16], replicated, may hold values from -0.59765625 to 0.59765625
- gate_weight: bfloat16 [16, 2880, 2880], P('dp', None, 'tensor'), may hold values from -0.109375 to 0.109375
- gate_bias: bfloat16 [16, 2880], P('dp', 'tensor'), may hold values from -0.59765625 to 0.59765625
- up_weight: bfloat16 [16, 2880, 2880], P('dp', None, 'tensor'), may hold values from -0.109375 to 0.109375
- up_bias: bfloat16 [16, 2880], P('dp', 'tensor'), may hold values from -0.59765625 to 0.59765625
- down_weight: bfloat16 [16, 2880, 2880], P('dp', 'tensor'), may hold values from -0.21875 to 0.21875
- down_bias: bfloat16 [16, 2880], P('dp'), may hold values from -0.59765625 to 0.59765625
- routes: int32 [2048, 4], P('dp'), may hold values from 0 to 15, all different within a row; in each aligned block of 128 rows (0 to 127, 128 to 255, ...) at most 64 rows name the same one
- lengths: int32 [3], replicated, may hold values from 1 to 1920, as said below
- cotangent: bfloat16 [2048, 2880], P('dp'), may hold values from -6 to 6
Outputs:
- block_out: float32 [2048, 2880], P('dp')
- grad_input: float32 [2048, 2880], P('dp')
- grad_attn_gain: float32 [2880], P('dp')
- grad_query_weight: float32 [2880, 4096], P('dp', 'tensor')
- grad_query_bias: float32 [4096], P('tensor')
- grad_key_weight: float32 [2880, 512], P('dp', 'tensor')
- grad_key_bias: float32 [512], P('tensor')
- grad_value_weight: float32 [2880, 512], P('dp', 'tensor')
- grad_value_bias: float32 [512], P('tensor')
- grad_attn_sinks: float32 [64], P('tensor')
- grad_out_weight: float32 [2880, 4096], P('dp', 'tensor')
- grad_out_bias: float32 [2880], P('dp')
- grad_mlp_gain: float32 [2880], P('dp')
- grad_router_weight: float32 [2880, 16], P('dp')
- grad_router_bias: float32 [16], replicated
- grad_gate_weight: float32 [16, 2880, 2880], P('dp', None, 'tensor')
- grad_gate_bias: float32 [16, 2880], P('dp', 'tensor')
- grad_up_weight: float32 [16, 2880, 2880], P('dp', None, 'tensor')
- grad_up_bias: float32 [16, 2880], P('dp', 'tensor')
- grad_down_weight: float32 [16, 2880, 2880], P('dp', 'tensor')
- grad_down_bias: float32 [16, 2880], P('dp')
The draws below stay inside these ranges and needn't reach their ends.
Inputs may be any that keep to these rules, and one draw needn't show every extreme that they name: `lengths`: 3 sequences packed in order; the first and the last together hold 128 tokens, and the middle one holds the other 2048 - 128.
All inputs are finite; a program needn't handle non-finite values.
Results may differ from the reference program's by a relative error of at most 0.024.
Values may be sent and summed in bfloat16 or wider, within the bound.
No kernel may reach another device: no remote copies, remote signals or barrier semaphores. Data moves between devices by JAX's collectives and lax.ppermute only.
A program may use at most 192 MiB of HBM per device.

```python
import math
from functools import partial
import jax
import jax.numpy as jnp
import numpy as np
from jax import lax

MODEL_DIM = 2880
QUERY_HEADS = 64
KEY_VALUE_HEADS = 8
HEAD_DIM = 64
FF = 2880
TOP = 4
WINDOW_KEYS = 128
TOK_DEV = 128
EXPERTS = 16
TOKEN_TOTAL = 2048
CAP = 64
N_DP = 16


def draw_lengths(key, part):
    key = jax.random.fold_in(key, 11)
    head_len = jax.random.randint(key, (), 1, TOK_DEV)
    tail_len = TOK_DEV - head_len
    return jnp.stack([head_len, TOKEN_TOTAL - TOK_DEV + 0 * head_len, tail_len]).astype(jnp.int32)


def shard_levels(key, extent, split, smallest, high):
    def one(dim, shards_of):
        steps = jax.random.uniform(jax.random.fold_in(jax.random.fold_in(key, 6), dim), (shards_of,), jnp.float32, smallest / len(split), high / len(split))
        return jnp.repeat(jnp.exp(steps), extent[dim] // shards_of).reshape((-1,) + (1,) * (len(extent) - dim - 1))

    level = one(*split[0])
    for cut in split[1:]:
        level = level * one(*cut)
    return level


def assign_block(stream_key, own, number, rows, number_of, top, most, lean):
    sequence = jax.random.permutation(stream_key, number_of)
    crowded, ordinary = shares(number_of, rows * top, most, lean, True), shares(number_of, rows * top, most, lean, False)
    places = jnp.arange(number_of)

    def named(tallies, offset_by):
        used = int((tallies > 0).sum())
        fixed = max(1, used // 4)
        shifted = fixed + (places - fixed + offset_by * (used - fixed)) % max(1, number_of - fixed)
        return jnp.zeros((number_of,), jnp.int32).at[sequence[jnp.where(places < fixed, places, shifted)]].set(jnp.asarray(tallies, jnp.int32))

    tallies = jnp.where(number % 4 == 0, named(crowded, number // 4), named(ordinary, number - number // 4 - 1))
    mixed = jax.random.permutation(jax.random.fold_in(own, 3), number_of)
    source_of, sink = mixed[0:number_of // 2 * 2:2], mixed[1:number_of // 2 * 2:2]
    room = jnp.minimum(tallies[source_of] - 1, most - tallies[sink]) // 2
    room = jnp.where((source_of == sequence[0]) | (sink == sequence[0]) | (tallies[sink] == 0), 0, jnp.maximum(room, 0))
    shifted = jax.random.randint(jax.random.fold_in(own, 4), (number_of // 2,), 0, 1 << 20) % (room + 1)
    tallies = tallies.at[source_of].add(-shifted).at[sink].add(shifted)
    items = jnp.searchsorted(jnp.cumsum(tallies), jnp.arange(rows * top), side="right").astype(jnp.int32)
    grid = items.reshape(top, rows).T
    grid = grid[jax.random.permutation(jax.random.fold_in(own, 1), rows)]
    offset_by = jax.random.randint(jax.random.fold_in(own, 2), (rows, 1), 0, top)
    return jnp.take_along_axis(grid, (jnp.arange(top)[None, :] + offset_by) % top, axis=1)


def shares(count, total, reach, slope, full):
    portions = [(1 << 20) // math.isqrt(grade ** slope) + 1 for grade in range(1, count + 1)]
    largest = reach if full else min(reach, max(-(-total // count), total * portions[0] // sum(portions)))
    least = 1 if total - largest >= count - 1 else 0
    given, rest = [largest] + [least] * (count - 1), total - largest - least * (count - 1)
    while rest > 0:
        candidates = [i for i in range(1, count) if given[i] < largest] or [i for i in range(1, count) if given[i] < reach]
        mass, budget = sum([portions[i] for i in candidates]), rest
        for i in candidates:
            extra = min(reach - given[i], max(1, budget * portions[i] // mass), rest)
            given[i] = given[i] + extra
            rest = rest - extra
    return np.array(given)


def gaussian(key, shape, width, most, cuts=(), kind=jnp.bfloat16):
    values = jax.random.normal(key, shape, jnp.float32) * width
    if len(cuts) > 0:
        values = shard_levels(key, shape, cuts, -0.22, 0.18) * values
    return jnp.clip(values, min=-most, max=most).astype(kind)


def setup_inputs(seed: int = 0) -> dict:
    seeds = jax.random.split(jax.random.key(seed), 24)
    residual = gaussian(seeds[0], (TOKEN_TOTAL, MODEL_DIM), 1.0, 6.0, ((0, 16),))
    attn_gain = jnp.clip(1.0 + 0.1 * jax.random.normal(seeds[1], (MODEL_DIM,), jnp.float32), 0.5, 1.5).astype(jnp.bfloat16)
    query_weight = gaussian(seeds[2], (MODEL_DIM, QUERY_HEADS * HEAD_DIM), MODEL_DIM ** -0.5, 0.109375, ((0, 16), (1, 8)))
    query_bias = gaussian(seeds[3], (QUERY_HEADS * HEAD_DIM,), 0.1, 0.59765625, ((0, 8),))
    key_matrix = gaussian(seeds[4], (MODEL_DIM, KEY_VALUE_HEADS * HEAD_DIM), MODEL_DIM ** -0.5, 0.109375, ((0, 16), (1, 8)))
    key_offset_bias = gaussian(seeds[5], (KEY_VALUE_HEADS * HEAD_DIM,), 0.1, 0.59765625, ((0, 8),))
    value_matrix = gaussian(seeds[6], (MODEL_DIM, KEY_VALUE_HEADS * HEAD_DIM), MODEL_DIM ** -0.5, 0.109375, ((0, 16), (1, 8)))
    value_offset_bias = gaussian(seeds[7], (KEY_VALUE_HEADS * HEAD_DIM,), 0.1, 0.59765625, ((0, 8),))
    attention_sink_logits = gaussian(seeds[8], (QUERY_HEADS,), 1.0, 3.0, ((0, 8),))
    out_weight = gaussian(seeds[9], (MODEL_DIM, QUERY_HEADS * HEAD_DIM), (QUERY_HEADS * HEAD_DIM // WINDOW_KEYS) ** -0.5, 1.0, ((0, 16), (1, 8)))
    out_bias = gaussian(seeds[10], (MODEL_DIM,), 0.1, 0.59765625, ((0, 16),))
    mlp_gain = jnp.clip(1.0 + 0.1 * jax.random.normal(seeds[11], (MODEL_DIM,), jnp.float32), 0.5, 1.5).astype(jnp.bfloat16)
    router_weight = gaussian(seeds[12], (MODEL_DIM, EXPERTS), (4 * MODEL_DIM) ** -0.5, 0.0546875, ((0, 16),))
    router_bias = gaussian(seeds[13], (EXPERTS,), 0.1, 0.59765625)
    gate_weight = gaussian(seeds[14], (EXPERTS, MODEL_DIM, FF), MODEL_DIM ** -0.5, 0.109375, ((0, 16), (2, 8)))
    gate_bias = gaussian(seeds[15], (EXPERTS, FF), 0.1, 0.59765625, ((0, 16), (1, 8)))
    up_weight = gaussian(seeds[16], (EXPERTS, MODEL_DIM, FF), MODEL_DIM ** -0.5, 0.109375, ((0, 16), (2, 8)))
    up_bias = gaussian(seeds[17], (EXPERTS, FF), 0.1, 0.59765625, ((0, 16), (1, 8)))
    down_weight = gaussian(seeds[18], (EXPERTS, FF, MODEL_DIM), (FF // 4) ** -0.5, 0.21875, ((0, 16), (1, 8)))
    down_bias = gaussian(seeds[19], (EXPERTS, MODEL_DIM), 0.1, 0.59765625, ((0, 16),))
    routes_keys = jax.random.split(jax.random.fold_in(seeds[20], 1), TOKEN_TOTAL // TOK_DEV)
    routes_turns = jax.random.permutation(jax.random.fold_in(seeds[20], 3), TOKEN_TOTAL // TOK_DEV)
    routes = jax.vmap(lambda own, number: assign_block(jax.random.fold_in(seeds[20], 2), own, number, TOK_DEV, EXPERTS, TOP, CAP, 2))(routes_keys, routes_turns).reshape((TOKEN_TOTAL, TOP))
    lengths = draw_lengths(jax.random.fold_in(seeds[23], 71), 0)
    cotangent = gaussian(seeds[22], (TOKEN_TOTAL, MODEL_DIM), 1.0, 6.0, ((0, 16),))
    return {"residual": residual, "attn_gain": attn_gain, "query_weight": query_weight, "query_bias": query_bias, "key_matrix": key_matrix, "key_offset_bias": key_offset_bias, "value_matrix": value_matrix, "value_offset_bias": value_offset_bias, "attention_sink_logits": attention_sink_logits, "out_weight": out_weight, "out_bias": out_bias, "mlp_gain": mlp_gain, "router_weight": router_weight, "router_bias": router_bias, "gate_weight": gate_weight, "gate_bias": gate_bias, "up_weight": up_weight, "up_bias": up_bias, "down_weight": down_weight, "down_bias": down_bias, "routes": routes, "lengths": lengths, "cotangent": cotangent}


@jax.custom_vjp
def lowered_precision(v):
    return lax.optimization_barrier(v.astype(jnp.bfloat16)).astype(jnp.float32)

@jax.custom_vjp
def lowered_precision_back(v):
    return v

def low_keep(v):
    return (lowered_precision(v), None)

def low_pass(kept, grad):
    return (grad,)

def back_keep(v):
    return (v, None)

def back_low(kept, grad):
    return (lowered_precision(grad),)
lowered_precision.defvjp(low_keep, low_pass)
lowered_precision_back.defvjp(back_keep, back_low)
PRECISE = lax.Precision.HIGHEST
EPSILON = 1e-05
ROPE_BASE = 150000.0
MASKED = -1000000000.0

def matrix_product(left_in, right_in):
    return jnp.dot(left_in, right_in, precision=PRECISE)

def rms_norm(values_in, gain_row):
    return values_in * lax.rsqrt(lax.optimization_barrier(jnp.mean(values_in * values_in, axis=-1, keepdims=True)) + EPSILON) * gain_row

def rope_table(position, head_width):
    half_width = head_width // 2
    frequency = ROPE_BASE ** (-2.0 * jnp.arange(half_width, dtype=jnp.float32) / head_width)
    angle_grid = position.astype(jnp.float32)[:, None] * frequency[None, :]
    return (jnp.cos(angle_grid), jnp.sin(angle_grid))

def apply_rotary(heads_in, cosine_values, sine_values):
    half_width = heads_in.shape[-1] // 2
    first_half = heads_in[..., :half_width]
    second_half = heads_in[..., half_width:]
    cos_part = cosine_values[:, None, :]
    sin_part = sine_values[:, None, :]
    return jnp.concatenate([first_half * cos_part - second_half * sin_part, second_half * cos_part + first_half * sin_part], axis=-1)

def segments(lengths, token_index):
    seq_ends = jnp.cumsum(lengths)
    seq_starts = seq_ends - lengths
    segment = lax.optimization_barrier(jnp.sum((token_index[:, None] >= seq_ends[None, :]).astype(jnp.int32), axis=1))
    member = segment[:, None] == jnp.arange(lengths.shape[0], dtype=jnp.int32)[None, :]
    position = token_index - lax.optimization_barrier(jnp.sum(jnp.where(member, seq_starts[None, :], 0), axis=1))
    return (segment, position)

def attention(query_rows, every_key, every_value, attention_sink_logits, segment):
    rows_per_block = min(512, TOKEN_TOTAL)
    query_group_count = QUERY_HEADS // KEY_VALUE_HEADS
    padded_keys = jnp.concatenate([jnp.zeros((WINDOW_KEYS, KEY_VALUE_HEADS, HEAD_DIM), every_key.dtype), every_key], axis=0)
    padded_values = jnp.concatenate([jnp.zeros((WINDOW_KEYS, KEY_VALUE_HEADS, HEAD_DIM), every_value.dtype), every_value], axis=0)
    pad_segment = jnp.concatenate([jnp.full((WINDOW_KEYS,), -1, jnp.int32), segment], axis=0)
    head_sink_logit = attention_sink_logits.reshape(KEY_VALUE_HEADS, query_group_count)[:, :, None]

    def one_block(starting_row):
        query_row_block = lax.dynamic_slice_in_dim(query_rows, starting_row, rows_per_block, 0).reshape(rows_per_block, KEY_VALUE_HEADS, query_group_count, HEAD_DIM)
        rows_k = lax.dynamic_slice_in_dim(padded_keys, starting_row, rows_per_block + WINDOW_KEYS, 0)
        rows_v = lax.dynamic_slice_in_dim(padded_values, starting_row, rows_per_block + WINDOW_KEYS, 0)
        seg_query = lax.dynamic_slice_in_dim(segment, starting_row, rows_per_block, 0)
        seg_key = lax.dynamic_slice_in_dim(pad_segment, starting_row, rows_per_block + WINDOW_KEYS, 0)
        place_query = starting_row + jnp.arange(rows_per_block, dtype=jnp.int32)
        place_key = starting_row - WINDOW_KEYS + jnp.arange(rows_per_block + WINDOW_KEYS, dtype=jnp.int32)
        offset = place_query[:, None] - place_key[None, :]
        allowed = (seg_query[:, None] == seg_key[None, :]) & (offset >= 0) & (offset < WINDOW_KEYS)
        scores = lowered_precision_back(0.125 * jnp.einsum('bkgd,ckd->kgbc', query_row_block, rows_k, precision=PRECISE))
        scores = jnp.where(allowed[None, None], scores, MASKED)
        peak_score = jnp.maximum(lax.optimization_barrier(jnp.max(scores, axis=-1)), head_sink_logit)
        exp_scores = jnp.exp(scores - peak_score[..., None])
        denominator = lax.optimization_barrier(jnp.sum(exp_scores, axis=-1)) + jnp.exp(head_sink_logit - peak_score)
        probs = lowered_precision(exp_scores / denominator[..., None])
        mixed = jnp.einsum('kgbc,ckd->bkgd', probs, rows_v, precision=PRECISE)
        return mixed.reshape(rows_per_block, QUERY_HEADS * HEAD_DIM)
    block_starts = jnp.arange(TOKEN_TOTAL // rows_per_block, dtype=jnp.int32) * rows_per_block
    return lax.map(jax.checkpoint(one_block), block_starts).reshape(TOKEN_TOTAL, QUERY_HEADS * HEAD_DIM)

def forward(context, residual, attn_gain, query_weight, query_bias, key_matrix, key_offset_bias, value_matrix, value_offset_bias, attention_sink_logits, out_weight, out_bias, mlp_gain, router_weight, router_bias, gate_weight, gate_bias, up_weight, up_bias, down_weight, down_bias):
    routes, segment, position, table = context
    cosine_values, sine_values = rope_table(position, HEAD_DIM)
    first_input_half = lowered_precision(rms_norm(residual, attn_gain))
    query_rows = lowered_precision(apply_rotary(lowered_precision_back(matrix_product(first_input_half, query_weight) + query_bias).reshape(TOKEN_TOTAL, QUERY_HEADS, HEAD_DIM), cosine_values, sine_values))
    every_key = lowered_precision(apply_rotary(lowered_precision_back(matrix_product(first_input_half, key_matrix) + key_offset_bias).reshape(TOKEN_TOTAL, KEY_VALUE_HEADS, HEAD_DIM), cosine_values, sine_values))
    every_value = lowered_precision(lowered_precision_back(matrix_product(first_input_half, value_matrix) + value_offset_bias)).reshape(TOKEN_TOTAL, KEY_VALUE_HEADS, HEAD_DIM)
    heads_out = lowered_precision(lowered_precision_back(attention(query_rows, every_key, every_value, attention_sink_logits, segment)))
    branch = lowered_precision_back(jnp.dot(heads_out, out_weight.T, precision=PRECISE))
    hidden_state = residual + branch + out_bias
    second_in = lowered_precision(rms_norm(hidden_state, mlp_gain))
    logits = matrix_product(second_in, router_weight) + router_bias
    gate_probs = jax.nn.softmax(jnp.take_along_axis(logits, routes, axis=1), axis=-1)
    flat_gates = gate_probs.reshape(-1)

    def expert_step(running, pieces):
        slot_ids, w_gate, b_gate, w_up, b_up, w_down, b_down = pieces
        filled = slot_ids >= 0
        safe_slot = jnp.where(filled, slot_ids, 0)
        token_rows = safe_slot // TOP
        slot_rows = second_in[token_rows]
        gate_in = lowered_precision_back(matrix_product(slot_rows, w_gate) + b_gate)
        up_in = lowered_precision_back(matrix_product(slot_rows, w_up) + b_up)
        gate_c = 7.0 * jnp.tanh(gate_in / 7.0)
        up_c = 7.0 * jnp.tanh(up_in / 7.0)
        hidden = lowered_precision((up_c + 1.0) * gate_c * jax.nn.sigmoid(1.702 * gate_c))
        result = lowered_precision_back(matrix_product(hidden, w_down) + b_down)
        weight = jnp.where(filled, flat_gates[safe_slot], 0.0)
        return (running.at[token_rows].add(weight[:, None] * result), None)
    mixture, unused = lax.scan(jax.checkpoint(expert_step), jnp.zeros_like(residual), (table, gate_weight, gate_bias, up_weight, up_bias, down_weight, down_bias))
    return hidden_state + mixture

def reference(residual, attn_gain, query_weight, query_bias, key_matrix, key_offset_bias, value_matrix, value_offset_bias, attention_sink_logits, out_weight, out_bias, mlp_gain, router_weight, router_bias, gate_weight, gate_bias, up_weight, up_bias, down_weight, down_bias, routes, lengths, cotangent):
    token_index = jnp.arange(TOKEN_TOTAL, dtype=jnp.int32)
    segment, position = segments(lengths, token_index)
    flat_route = routes.reshape(-1)
    expert_ids = jnp.arange(EXPERTS, dtype=jnp.int32)
    onehot = (flat_route[:, None] == expert_ids[None, :]).astype(jnp.int32)
    ranking = lax.optimization_barrier(jnp.sum((jnp.cumsum(onehot, axis=0) - onehot) * onehot, axis=1))
    table = jnp.full((EXPERTS, N_DP * CAP), -1, jnp.int32).at[flat_route, ranking].set(jnp.arange(TOKEN_TOTAL * TOP, dtype=jnp.int32))
    floats = (residual.astype(jnp.float32), attn_gain.astype(jnp.float32), query_weight.astype(jnp.float32), query_bias.astype(jnp.float32), key_matrix.astype(jnp.float32), key_offset_bias.astype(jnp.float32), value_matrix.astype(jnp.float32), value_offset_bias.astype(jnp.float32), attention_sink_logits.astype(jnp.float32), out_weight.astype(jnp.float32), out_bias.astype(jnp.float32), mlp_gain.astype(jnp.float32), router_weight.astype(jnp.float32), router_bias.astype(jnp.float32), gate_weight.astype(jnp.float32), gate_bias.astype(jnp.float32), up_weight.astype(jnp.float32), up_bias.astype(jnp.float32), down_weight.astype(jnp.float32), down_bias.astype(jnp.float32))
    block_out, pull_back = jax.vjp(partial(forward, (routes, segment, position, table)), *floats)
    grads = pull_back(cotangent.astype(jnp.float32))
    return (block_out, grads[0], grads[1], grads[2], grads[3], grads[4], grads[5], grads[6], grads[7], grads[8], grads[9], grads[10], grads[11], grads[12], grads[13], grads[14], grads[15], grads[16], grads[17], grads[18], grads[19])
```

```python
import jax
import jax.numpy as jnp
from jax import lax
from jax.sharding import PartitionSpec as P

HEAD_DIM = 64
WINDOW_KEYS = 128
EPSILON = 1e-05
ROPE_BASE = 150000.0
MASKED = -1000000000.0
BF = jnp.bfloat16
F32 = jnp.float32


def rope_table(position, head_width):
    half_width = head_width // 2
    frequency = ROPE_BASE ** (-2.0 * jnp.arange(half_width, dtype=F32) / head_width)
    angle_grid = position.astype(F32)[:, None] * frequency[None, :]
    return (jnp.cos(angle_grid), jnp.sin(angle_grid))


def rotate(heads_in, cos, sin):
    half = heads_in.shape[-1] // 2
    a, b = heads_in[..., :half], heads_in[..., half:]
    c, s = cos[:, None, :], sin[:, None, :]
    return jnp.concatenate([a * c - b * s, b * c + a * s], axis=-1)


def segments(lengths, token_index):
    seq_ends = jnp.cumsum(lengths)
    seq_starts = seq_ends - lengths
    segment = jnp.sum((token_index[:, None] >= seq_ends[None, :]).astype(jnp.int32), axis=1)
    member = segment[:, None] == jnp.arange(lengths.shape[0], dtype=jnp.int32)[None, :]
    position = token_index - jnp.sum(jnp.where(member, seq_starts[None, :], 0), axis=1)
    return (segment, position)


def exchange(value, axis):
    return lax.all_to_all(value, axis, split_axis=0, concat_axis=0, tiled=True)


def spread(value, axis):
    count = lax.axis_size(axis)
    return exchange(jnp.broadcast_to(value[None], (count,) + value.shape), axis)


def dot(a, b, dims=((1,), (0,))):
    return lax.dot_general(a, b, (dims, ((), ())), preferred_element_type=F32)


def high_low(value):
    high = value.astype(BF)
    return high, (value - high.astype(F32)).astype(BF)


def local(
    residual,
    attn_gain,
    query_weight,
    query_bias,
    key_matrix,
    key_offset_bias,
    value_matrix,
    value_offset_bias,
    attention_sink_logits,
    out_weight,
    out_bias,
    mlp_gain,
    router_weight,
    router_bias,
    gate_weight,
    gate_bias,
    up_weight,
    up_bias,
    down_weight,
    down_bias,
    routes,
    lengths,
    cotangent,
):
    rows, width = residual.shape
    experts = router_weight.shape[1]
    dp = lax.axis_size("dp")
    tn = lax.axis_size("tensor")
    me_dp = lax.axis_index("dp")
    me_t = lax.axis_index("tensor")
    hd = HEAD_DIM
    window = WINDOW_KEYS
    q_heads = attention_sink_logits.shape[0]
    cap = 2 * rows * routes.shape[1] // experts
    chunk = width // dp
    chunk_pad = 192
    cols = 384
    wide = tn * cols
    spare = width - (tn - 1) * cols
    slots = experts * cap

    def padded(a):
        return jnp.pad(a, ((0, 0), (0, wide - width)))

    def my_cols(a):
        return lax.dynamic_slice_in_dim(a, me_t * cols, cols, 1)

    def by_chunk(a):
        a = jnp.pad(a.reshape(rows, dp, chunk), ((0, 0), (0, 0), (0, chunk_pad - chunk)))
        a = a.transpose(1, 0, 2)
        return jnp.concatenate([a[:, : rows // 2], a[:, rows // 2 :]], axis=2)

    def of_chunk(a):
        first = a[:, :, :chunk].reshape(dp * rows // 2, chunk)
        second = a[:, :, chunk_pad : chunk_pad + chunk].reshape(dp * rows // 2, chunk)
        return first, second

    expert_ids = jnp.arange(experts, dtype=jnp.int32)
    member = jnp.any(routes[:, :, None] == expert_ids[None, None, :], axis=1)
    member_f = member.astype(F32)
    below = (jnp.arange(rows)[:, None] > jnp.arange(rows)[None, :]).astype(BF)
    rank = dot(below, member.astype(BF)).astype(jnp.int32)
    place = (
        (rank.T[:, None, :] == jnp.arange(cap, dtype=jnp.int32)[None, :, None])
        & member.T[:, None, :]
    ).astype(BF)
    place2 = place.reshape(slots, rows)

    extras = jnp.concatenate(
        [attn_gain[None], mlp_gain[None], out_bias[None], router_weight.T, jnp.zeros((2, chunk), BF)]
    ).reshape(7, 3, chunk)
    extras = jnp.pad(extras, ((0, 0), (0, 0), (0, chunk_pad - chunk))).reshape(7, 3 * chunk_pad)
    own_qkv = jnp.concatenate([query_weight, key_matrix, value_matrix], axis=1)
    qkv_cols = own_qkv.shape[1]
    extras = jnp.pad(extras, ((0, chunk_pad - chunk - 7), (0, qkv_cols - 3 * chunk_pad)))
    qkv_all = lax.all_gather(jnp.concatenate([own_qkv, extras], axis=0), "dp")
    out_all = lax.all_gather(
        jnp.pad(out_weight, ((0, chunk_pad - chunk), (0, 0))), "dp"
    )
    small = (
        qkv_all[:, chunk : chunk + 7, : 3 * chunk_pad]
        .reshape(dp, 21, chunk_pad)[:, :, :chunk]
        .transpose(1, 0, 2)
        .reshape(21, width)
    )
    gain_one = small[0].astype(F32)
    gain_two = small[1].astype(F32)
    bias_out = small[2].astype(F32)
    router_t = small[3 : 3 + experts]

    inputs = residual.astype(F32)
    scale_one = lax.rsqrt(jnp.mean(inputs * inputs, axis=-1, keepdims=True) + EPSILON)
    normed_one = inputs * scale_one
    grad_ext = jnp.concatenate(
        [cotangent, member.astype(BF), jnp.zeros((rows, wide - width - experts), BF)], axis=1
    )
    grad_slots = dot(place2, my_cols(grad_ext)).astype(BF).reshape(experts, cap, cols)
    first_got = exchange(
        jnp.concatenate([grad_slots, by_chunk(normed_one.astype(BF))], axis=1), "dp"
    )
    grad_rows = lax.all_gather(first_got[:, :cap].reshape(slots, cols), "tensor")
    grad_rows = grad_rows.transpose(1, 0, 2).reshape(slots, wide)
    first_chunk = tuple(
        (half.astype(F32) * attn_gain.astype(F32)[None]).astype(BF)
        for half in of_chunk(first_got[:, cap:])
    )

    starting_row = me_dp * rows
    token_index = starting_row + jnp.arange(rows, dtype=jnp.int32)
    segment, position = segments(lengths, token_index)
    key_index = starting_row - window + jnp.arange(rows + window, dtype=jnp.int32)
    key_segment, unused = segments(lengths, key_index)
    offset = token_index[:, None] - key_index[None, :]
    allowed = (
        (segment[:, None] == key_segment[None, :])
        & (offset >= 0)
        & (offset < window)
        & (key_index[None, :] >= 0)
    )
    cos, sin = rope_table(position, hd)
    normed_pad = jnp.pad(
        normed_one.reshape(rows, dp, chunk), ((0, 0), (0, 0), (0, chunk_pad - chunk))
    )
    gain_pad = qkv_all[:, chunk, :chunk_pad].astype(F32)
    first_in = (normed_pad * gain_pad[None]).astype(BF).reshape(rows, dp * chunk_pad)
    qkv_bias = jnp.concatenate([query_bias, key_offset_bias, value_offset_bias]).astype(F32)
    lin = dot(first_in, qkv_all.reshape(dp * chunk_pad, qkv_cols)) + qkv_bias
    q_cols = q_heads * hd
    query = rotate(lin[:, :q_cols].reshape(rows, q_heads, hd), cos, sin).astype(BF)
    key_own = rotate(lin[:, None, q_cols : q_cols + hd], cos, sin).astype(BF)[:, 0]
    value_own = lin[:, q_cols + hd :].astype(BF)
    own_kv = jnp.concatenate([key_own, value_own], axis=1)
    rim_kv = lax.ppermute(own_kv, "dp", [(i, i + 1) for i in range(dp - 1)])
    keys = jnp.concatenate([rim_kv[:, :hd], key_own], axis=0)
    values = jnp.concatenate([rim_kv[:, hd:], value_own], axis=0)
    scores = 0.125 * jnp.einsum("rgd,cd->grc", query, keys, preferred_element_type=F32)
    scores = jnp.where(allowed[None], scores, MASKED)
    sink = attention_sink_logits.astype(F32)[:, None]
    peak = jnp.maximum(jnp.max(scores, axis=-1), sink)
    exp_scores = jnp.exp(scores - peak[..., None])
    sink_exp = jnp.exp(sink - peak)
    denom = jnp.sum(exp_scores, axis=-1) + sink_exp
    probs = exp_scores / denom[..., None]
    sink_prob = sink_exp / denom
    prob_low = probs.astype(BF)
    heads_out = (
        jnp.einsum("grc,cd->rgd", prob_low, values, preferred_element_type=F32)
        .astype(BF)
        .reshape(rows, q_cols)
    )
    heads_all = lax.all_gather(heads_out, "dp")
    out_full = out_all[:, :chunk].reshape(width, q_cols)

    branch = padded(dot(heads_out, out_full, ((1,), (1,))).astype(BF))
    branch = exchange(branch.reshape(rows, tn, cols).transpose(1, 0, 2), "tensor")
    branch = jnp.sum(branch.astype(F32), axis=0)
    hidden_cols = my_cols(padded(inputs + bias_out[None])) + branch
    gain_cols = lax.dynamic_slice_in_dim(jnp.pad(gain_two, (0, wide - width)), me_t * cols, cols, 0)
    out_rows = dot(place2, (hidden_cols * gain_cols[None]).astype(BF)).astype(BF)
    expert_cols = exchange(out_rows.reshape(experts, cap, cols), "dp").reshape(slots, cols)
    expert_in = lax.all_gather(expert_cols, "tensor")
    expert_in = expert_in.transpose(1, 0, 2).reshape(slots, wide)[:, :width]

    hidden_state = (
        spread(hidden_cols.astype(BF), "tensor")
        .transpose(1, 0, 2)
        .reshape(rows, wide)[:, :width]
        .astype(F32)
    )
    scale_two = lax.rsqrt(jnp.mean(hidden_state * hidden_state, axis=-1, keepdims=True) + EPSILON)
    normed_two = hidden_state * scale_two
    second_in = (normed_two * gain_two).astype(BF)
    bias_router = router_bias.astype(F32)

    def gates_of(logits, chosen):
        top = jnp.max(jnp.where(chosen > 0, logits, MASKED), axis=-1, keepdims=True)
        weights = jnp.where(chosen > 0, jnp.exp(logits - top), 0.0)
        total = jnp.sum(weights, axis=-1, keepdims=True)
        return weights / jnp.where(total > 0, total, 1.0)

    gates = gates_of(dot(second_in, router_t, ((1,), (1,))) + bias_router, member_f)

    w_gate, w_up, w_down = gate_weight[0], up_weight[0], down_weight[0]
    grads_in = grad_rows[:, :width]
    chosen = grad_rows[:, width : width + experts].astype(F32)
    down_back = dot(grads_in, w_down, ((1,), (1,)))
    square = jnp.square(expert_in.astype(F32) / gain_two[None])
    row_scale = lax.rsqrt(jnp.mean(square, axis=-1, keepdims=True) + EPSILON)
    row_gates = gates_of(
        row_scale * dot(expert_in, router_t, ((1,), (1,))) + bias_router, chosen
    )
    mine = (expert_ids == me_dp).astype(F32)
    gate_of_row = jnp.sum(row_gates * mine[None], axis=-1, keepdims=True)
    gate_in = row_scale * dot(expert_in, w_gate) + gate_bias[0].astype(F32)
    up_in = row_scale * dot(expert_in, w_up) + up_bias[0].astype(F32)
    gate_tanh = jnp.tanh(gate_in / 7.0)
    up_tanh = jnp.tanh(up_in / 7.0)
    gate_c = 7.0 * gate_tanh
    up_c = 7.0 * up_tanh
    sigma = jax.nn.sigmoid(1.702 * gate_c)
    glu = gate_c * sigma
    hidden = ((up_c + 1.0) * glu).astype(BF)
    bias_down = down_bias[0].astype(F32)
    bias_on = (me_t == 0).astype(F32)
    act_grad = gate_of_row * down_back
    gate_grad = (
        act_grad
        * (up_c + 1.0)
        * (sigma + 1.702 * gate_c * sigma * (1.0 - sigma))
        * (1.0 - gate_tanh * gate_tanh)
    ).astype(BF)
    up_grad = (act_grad * glu * (1.0 - up_tanh * up_tanh)).astype(BF)
    gates_part = jnp.sum(hidden.astype(F32) * down_back, axis=-1, keepdims=True) + bias_on * dot(
        grads_in, down_bias[0][:, None]
    )
    rows_back = dot(gate_grad, w_gate, ((1,), (1,))) + dot(up_grad, w_up, ((1,), (1,)))
    gates_high, gates_low = high_low(gates_part)
    rows_back = jnp.concatenate(
        [
            rows_back.astype(BF),
            gates_high,
            gates_low,
            jnp.zeros((slots, wide - width - 2), BF),
        ],
        axis=1,
    )

    def summed(value):
        got = exchange(value.reshape(slots, tn, cols).transpose(1, 0, 2), "tensor")
        return jnp.sum(got.astype(F32), axis=0)

    back_cols = summed(rows_back)
    gates_high, gates_low = high_low(back_cols[:, spare + 0 : spare + 1] + back_cols[:, spare + 1 : spare + 2])
    last = (me_t == tn - 1).astype(BF)
    back_low = back_cols.astype(BF)
    back_low = jnp.concatenate(
        [
            back_low[:, :spare],
            jnp.where(me_t == tn - 1, gates_high, back_low[:, spare : spare + 1]),
            jnp.where(me_t == tn - 1, gates_low, back_low[:, spare + 1 : spare + 2]),
            back_low[:, spare + 2 :],
        ],
        axis=1,
    )
    back_got = exchange(back_low.reshape(experts, cap, cols), "dp")
    back_tokens = dot(place2, back_got.reshape(slots, cols), ((0,), (0,))).astype(BF)
    gates_back = jnp.einsum(
        "ers,erk->ske", place, back_got[:, :, spare : spare + 2], preferred_element_type=F32
    ).astype(BF).reshape(rows, 2 * experts)
    back_tokens = jnp.where(
        me_t == tn - 1,
        jnp.concatenate(
            [
                back_tokens[:, :spare],
                gates_back,
                jnp.zeros((rows, cols - spare - 2 * experts), BF),
            ],
            axis=1,
        ),
        back_tokens,
    )
    back_all = spread(back_tokens, "tensor").transpose(1, 0, 2).reshape(rows, wide)
    gate_grads = back_all[:, width : width + experts].astype(F32) + back_all[
        :, width + experts : width + 2 * experts
    ].astype(F32)
    logit_grad = gates * (gate_grads - jnp.sum(gates * gate_grads, axis=-1, keepdims=True))
    second_grad = back_all[:, :width].astype(F32) + dot(logit_grad.astype(BF), router_t)
    grad_router = dot(logit_grad.astype(BF), second_in, ((0,), (0,)))
    grad_router_bias = jnp.sum(logit_grad, axis=0)

    grad_out = cotangent.astype(F32)
    scaled = second_grad * gain_two
    state_grad = grad_out + scale_two * (
        scaled - normed_two * jnp.mean(scaled * normed_two, axis=-1, keepdims=True)
    )
    grad_mlp_gain = jnp.sum(second_grad * normed_two, axis=0)
    state_low = state_grad.astype(BF)
    heads_grad = dot(state_low, out_full).astype(BF).reshape(rows, q_heads, hd)

    prob_grad = jnp.einsum("rgd,cd->grc", heads_grad, values, preferred_element_type=F32)
    row_delta = jnp.sum(probs * prob_grad, axis=-1)
    score_grad = (probs * (prob_grad - row_delta[..., None])).astype(BF)
    grad_sinks = -jnp.sum(sink_prob * row_delta, axis=-1)
    query_grad = 0.125 * jnp.einsum("grc,cd->rgd", score_grad, keys, preferred_element_type=F32)
    keys_grad = 0.125 * jnp.einsum("grc,rgd->cd", score_grad, query, preferred_element_type=F32)
    values_grad = jnp.einsum("grc,rgd->cd", prob_low, heads_grad, preferred_element_type=F32)
    kv_grad = jnp.concatenate([keys_grad, values_grad], axis=1)
    rim_grad = lax.ppermute(
        kv_grad[:window].astype(BF), "dp", [(i + 1, i) for i in range(dp - 1)]
    )
    kv_grad = kv_grad[window:] + rim_grad.astype(F32)
    lin_grad = jnp.concatenate(
        [
            rotate(query_grad, cos, -sin).reshape(rows, q_cols),
            rotate(kv_grad[:, None, :hd], cos, -sin)[:, 0],
            kv_grad[:, hd:],
        ],
        axis=1,
    ).astype(BF)

    sink_rows = jnp.pad(
        jnp.stack(high_low(grad_sinks)), ((0, 14), (0, qkv_cols - q_heads))
    )
    lin_all = lax.all_gather(jnp.concatenate([lin_grad, sink_rows], axis=0), "dp")
    half = rows // 2
    lin_first = lin_all[:, :half].reshape(dp * half, qkv_cols)
    lin_second = lin_all[:, half:rows].reshape(dp * half, qkv_cols)
    grad_qkv = dot(first_chunk[0], lin_first, ((0,), (0,))) + dot(
        first_chunk[1], lin_second, ((0,), (0,))
    )
    grad_bias = jnp.sum(lin_all[:, :rows].astype(F32), axis=(0, 1))
    grad_sinks = jnp.sum(lin_all[:, rows : rows + 2, :q_heads].astype(F32), axis=(0, 1))

    qkv_full = qkv_all[:, :chunk].reshape(width, qkv_cols)
    first_part = dot(lin_grad, qkv_full, ((1,), (1,))).astype(BF)
    own_rows = rows // tn
    first_rows = jnp.sum(
        exchange(first_part.reshape(tn, own_rows, width), "tensor").astype(F32), axis=0
    )

    def my_rows(a):
        return lax.dynamic_slice_in_dim(a, me_t * own_rows, own_rows, 0)

    normed_mine = my_rows(normed_one)
    scaled_one = first_rows * gain_one
    grad_rows_mine = my_rows(state_grad) + my_rows(scale_one) * (
        scaled_one - normed_mine * jnp.mean(scaled_one * normed_mine, axis=-1, keepdims=True)
    )
    gain_part = jnp.sum(own_qkv.astype(F32) * grad_qkv, axis=1)
    gain_rows = jnp.pad(jnp.stack(high_low(gain_part)), ((0, 14), (0, width - chunk)))
    input_all = spread(jnp.concatenate([grad_rows_mine.astype(BF), gain_rows], axis=0), "tensor")
    grad_input = input_all[:, :own_rows].reshape(rows, width).astype(F32)
    grad_attn_gain = jnp.sum(
        input_all[:, own_rows : own_rows + 2, :chunk].astype(F32), axis=(0, 1)
    ) / attn_gain.astype(F32)

    down_out = gate_of_row * (dot(hidden, w_down) + bias_on * bias_down)
    mixed_cols = summed(padded(down_out.astype(BF))).astype(BF).reshape(experts, cap, cols)
    vectors = jnp.concatenate([grad_router, grad_mlp_gain[None], jnp.zeros((1, width), F32)])
    vectors = jnp.pad(
        vectors.astype(BF).reshape(9, 2, dp, chunk), ((0, 0), (0, 0), (0, 0), (0, chunk_pad - chunk))
    )
    vectors = vectors.transpose(2, 0, 1, 3).reshape(dp, 9, 2 * chunk_pad)
    bias_row = jnp.pad(jnp.concatenate(high_low(grad_router_bias)), (0, cols - 2 * experts))
    bias_row = jnp.broadcast_to(bias_row[None, None], (dp, 1, cols))
    last_got = exchange(
        jnp.concatenate(
            [mixed_cols, by_chunk(state_low), vectors, bias_row, jnp.zeros((dp, 6, cols), BF)], axis=1
        ),
        "dp",
    )
    mixture = dot(place2, last_got[:, :cap].reshape(slots, cols), ((0,), (0,))).astype(BF)
    mixture = spread(mixture, "tensor").transpose(1, 0, 2).reshape(rows, wide)[:, :width]
    block_out = hidden_state + mixture.astype(F32)

    state_chunk = of_chunk(last_got[:, cap : cap + half])
    heads_first = heads_all[:, :half].reshape(dp * half, q_cols)
    heads_second = heads_all[:, half:].reshape(dp * half, q_cols)
    grad_out_weight = dot(state_chunk[0], heads_first, ((0,), (0,))) + dot(
        state_chunk[1], heads_second, ((0,), (0,))
    )
    grad_out_bias = jnp.sum(state_chunk[0].astype(F32), axis=0) + jnp.sum(
        state_chunk[1].astype(F32), axis=0
    )
    sums = jnp.sum(last_got[:, cap + half :].astype(F32), axis=0)
    vectors = sums[:9].reshape(18, chunk_pad)[:, :chunk]
    grad_router_weight = vectors[:experts].T
    grad_mlp_gain = vectors[experts]
    grad_router_bias = sums[9, :experts] + sums[9, experts : 2 * experts]

    low_gate = (row_scale * gate_grad.astype(F32)).astype(BF)
    low_up = (row_scale * up_grad.astype(F32)).astype(BF)
    grad_gate_weight = dot(expert_in, low_gate, ((0,), (0,)))
    grad_up_weight = dot(expert_in, low_up, ((0,), (0,)))
    grad_gate_bias = jnp.sum(gate_grad.astype(F32), axis=0)
    grad_up_bias = jnp.sum(up_grad.astype(F32), axis=0)
    low_hidden = (gate_of_row * hidden.astype(F32)).astype(BF)
    grad_down_weight = dot(low_hidden, grads_in, ((0,), (0,)))
    gate_rows = jnp.concatenate(high_low(gate_of_row), axis=1)
    grad_down_bias = jnp.sum(dot(gate_rows, grads_in, ((0,), (0,))), axis=0)

    return (
        block_out,
        grad_input,
        grad_attn_gain,
        grad_qkv[:, :q_cols],
        grad_bias[:q_cols],
        grad_qkv[:, q_cols : q_cols + hd],
        grad_bias[q_cols : q_cols + hd],
        grad_qkv[:, q_cols + hd :],
        grad_bias[q_cols + hd :],
        grad_sinks,
        grad_out_weight,
        grad_out_bias,
        grad_mlp_gain,
        grad_router_weight,
        grad_router_bias,
        grad_gate_weight[None],
        grad_gate_bias[None],
        grad_up_weight[None],
        grad_up_bias[None],
        grad_down_weight[None],
        grad_down_bias[None],
    )


def solution(mesh):
    return jax.shard_map(
        local,
        mesh=mesh,
        in_specs=(
            P("dp", None),
            P("dp"),
            P("dp", "tensor"),
            P("tensor"),
            P("dp", "tensor"),
            P("tensor"),
            P("dp", "tensor"),
            P("tensor"),
            P("tensor"),
            P("dp", "tensor"),
            P("dp"),
            P("dp"),
            P("dp", None),
            P(),
            P("dp", None, "tensor"),
            P("dp", "tensor"),
            P("dp", None, "tensor"),
            P("dp", "tensor"),
            P("dp", "tensor", None),
            P("dp", None),
            P("dp", None),
            P(),
            P("dp", None),
        ),
        out_specs=(
            P("dp", None),
            P("dp", None),
            P("dp"),
            P("dp", "tensor"),
            P("tensor"),
            P("dp", "tensor"),
            P("tensor"),
            P("dp", "tensor"),
            P("tensor"),
            P("tensor"),
            P("dp", "tensor"),
            P("dp"),
            P("dp"),
            P("dp", None),
            P(),
            P("dp", None, "tensor"),
            P("dp", "tensor"),
            P("dp", None, "tensor"),
            P("dp", "tensor"),
            P("dp", "tensor", None),
            P("dp", None),
        ),
        check_vma=False,
    )
```

```python
import functools

import jax
import jax.numpy as jnp
from jax import lax
from jax.experimental import pallas as pl
from jax.experimental.pallas import tpu as pltpu
from jax.sharding import PartitionSpec as P

HEAD_DIM = 64
HALF = HEAD_DIM // 2
WINDOW = 128
EPSILON = 1e-05
ROPE_BASE = 150000.0
MASKED = -1000000000.0
BF = jnp.bfloat16
F32 = jnp.float32

ROWS = 128
WIDTH = 2880
EXPERTS = 16
CAP = 64
SLOTS = EXPERTS * CAP
DP = 16
TN = 8
CHUNK = WIDTH // DP
CPAD = 192
COLS = 384
WIDE = TN * COLS
SPARE = WIDTH - (TN - 1) * COLS
FF = 360
HEADS = 8
Q = HEADS * HEAD_DIM
QKV = Q + 2 * HEAD_DIM
CAT = HEADS * ROWS

VMEM = pl.BlockSpec(memory_space=pltpu.VMEM)
SMEM = pl.BlockSpec(memory_space=pltpu.SMEM)
ANY = pl.BlockSpec(memory_space=pl.ANY)
NN = ((1,), (0,))
NT = ((1,), (1,))
TNN = ((0,), (0,))


def dot(a, b, dims=NN):
    return lax.dot_general(a, b, (dims, ((), ())), preferred_element_type=F32)


def params(mib=48):
    return pltpu.CompilerParams(vmem_limit_bytes=mib << 20)


def cost(us):
    return pl.CostEstimate(flops=int(us * 1e9), bytes_accessed=int(us * 3.2e6), transcendentals=0)


def shape(dims, dtype):
    return pltpu.HBM(dims, dtype)


def held(a):
    return pltpu.with_memory_space_constraint(a, pltpu.HBM)


def call(body, outs, args, smem=0, scratch=(), after=(), us=3, mib=26, name=None):
    n = len(args)
    run = (lambda *refs: body(*refs[:n], *refs[n + len(after) :])) if after else body
    return pl.pallas_call(
        run,
        out_shape=outs,
        in_specs=[SMEM] * smem + [VMEM] * (n - smem) + [ANY] * len(after),
        out_specs=jax.tree.map(lambda _: VMEM, outs),
        scratch_shapes=list(scratch),
        compiler_params=params(mib),
        cost_estimate=cost(us),
        name=name,
    )(*args[:smem], *map(held, args[smem:]), *map(held, after))


def rows_mask(rows, first, second):
    n = first.shape[1]
    at = lax.broadcasted_iota(jnp.int32, (rows, n), 0)
    return jnp.where(at == 0, first, jnp.where(at == 1, second, 0.0))


def split(value):
    high = value.astype(BF).astype(F32)
    return high, value - high


def rotary(a, b, cos, sin):
    return a * cos - b * sin, b * cos + a * sin


def qkv_kernel(idx, wa, wb, x, x_rim, bias, cos, sin, cos_rim, sin_rim, q_out, kv_out, rim_out):
    acc = jnp.zeros((ROWS, QKV), F32)
    rim = jnp.zeros((ROWS, 2 * HEAD_DIM), F32)
    for k in range(8):
        for j, w in ((k, wa[k]), (8 + k, wb[k])):
            acc += dot(x[idx[j]], w, TNN)
            rim += dot(x_rim[idx[j]], w[:, Q:], TNN)
    lin = (acc + bias[...]).T.reshape(HEADS + 2, HEAD_DIM, ROWS)
    c, s = cos[...], sin[...]
    for h in range(HEADS):
        a, b = rotary(lin[h, :HALF], lin[h, HALF:], c, s)
        q_out[:HALF, h * ROWS : (h + 1) * ROWS] = a.astype(BF)
        q_out[HALF:, h * ROWS : (h + 1) * ROWS] = b.astype(BF)
    rim = (rim + bias[:, Q:]).T
    for out, k, v, c, s in (
        (kv_out, lin[HEADS], lin[HEADS + 1], c, s),
        (rim_out, rim[:HEAD_DIM], rim[HEAD_DIM:], cos_rim[...], sin_rim[...]),
    ):
        a, b = rotary(k[:HALF], k[HALF:], c, s)
        out[:HALF] = a.astype(BF)
        out[HALF:HEAD_DIM] = b.astype(BF)
        out[HEAD_DIM:] = v.astype(BF)


def attention_kernel(
    q, rim, own, mask, sink, w, prob_out, sinkp_out, heads_out, branch_out, ext_out, dense
):
    keys = jnp.concatenate([rim[:HEAD_DIM], own[:HEAD_DIM]], axis=1).astype(F32).T.astype(BF)
    values = jnp.concatenate([rim[HEAD_DIM:], own[HEAD_DIM:]], axis=1)
    allowed = jnp.concatenate([mask[...]] * HEADS, axis=1) > 0
    scores = jnp.where(allowed, 0.125 * dot(keys, q[...]), MASKED)
    peak = jnp.maximum(jnp.max(scores, axis=0, keepdims=True), sink[...])
    weights = jnp.exp(scores - peak)
    sink_exp = jnp.exp(sink[...] - peak)
    inverse = 1.0 / (jnp.sum(weights, axis=0, keepdims=True) + sink_exp)
    probs = weights * inverse
    prob_out[...] = probs
    sinkp_out[...] = sink_exp * inverse
    mixed = dot(values, probs.astype(BF)).astype(BF)
    for h in range(HEADS):
        heads_out[h * HEAD_DIM : (h + 1) * HEAD_DIM] = mixed[:, h * ROWS : (h + 1) * ROWS]
    heads = heads_out[...]
    dense[WIDTH:] = jnp.zeros((WIDE - WIDTH, ROWS), F32)
    ext_out[WIDTH:] = jnp.zeros((WIDE - WIDTH, ROWS), F32)
    for k in range(DP):
        dense[k * CHUNK : (k + 1) * CHUNK] = dot(w[k, :, :Q], heads)[:CHUNK]
        ext_out[k * CHUNK : (k + 1) * CHUNK] = w[k, :, Q:].astype(F32)[:CHUNK]
    branch_out[...] = dense[...].astype(BF)


def slice_kernel(at, got, residual, ext, place, hidden_out, rows_out):
    mine = pl.ds(pl.multiple_of(at[0] * COLS, COLS), COLS)
    total = residual[mine].astype(F32) + ext[mine, 1:2]
    for t in range(TN):
        total += got[t].astype(F32)
    for t in range(TN):
        hidden_out[t] = total.astype(BF)
    moved = (total * ext[mine, 0:1]).astype(BF)
    rows_out[...] = dot(place[...], moved, NT).astype(BF).reshape(rows_out.shape)


def masked_gates(logits, chosen):
    top = jnp.max(jnp.where(chosen > 0, logits, MASKED), axis=0, keepdims=True)
    weights = jnp.where(chosen > 0, jnp.exp(logits - top), 0.0)
    total = jnp.sum(weights, axis=0, keepdims=True)
    return weights / jnp.where(total > 0, total, 1.0)


def gates_kernel(hidden, ext, router, bias, member, scale_out, gates_out):
    h = hidden[...].astype(F32)[:WIDTH]
    scale = lax.rsqrt(jnp.sum(h * h, axis=0, keepdims=True) * (1.0 / WIDTH) + EPSILON)
    scale_out[...] = scale
    second = (h * scale * ext[:WIDTH, 0:1]).astype(BF)
    logits = dot(router[:, :WIDTH], second) + bias[...]
    gates_out[...] = masked_gates(logits, member[...])


def assemble(at, pieces, out):
    x00, x03, x01, x10, up2, down2, side2, up3, down3 = pieces
    half = COLS // 2

    def put(r, value, low=None):
        start = at[r] * COLS + (half if low is False else 0)
        rows = COLS if low is None else half
        out[pl.ds(pl.multiple_of(start, half), rows)] = value

    put(0, x00[...])
    put(3, x03[...])
    put(1, x01[...])
    put(4, x10[...])
    put(2, up2[0], True)
    put(7, up2[1], True)
    put(2, down2[0], False)
    put(5, down2[1], False)
    put(7, side2[0], False)
    put(5, side2[1], True)
    put(6, up3[...], True)
    put(6, down3[...], False)


def turn_kernel(got, out):
    out[...] = got[...].reshape(SLOTS, COLS).astype(F32).T.astype(BF)


def stack_kernel(*refs):
    for k, ref in enumerate(refs[:-1]):
        refs[-1][k] = ref[...]


def column(row, rows):
    n = row.shape[1]
    value = jnp.broadcast_to(row.astype(F32), (8, n)).T[:, 0:1]
    return value if n == rows else jnp.concatenate([value, jnp.zeros((rows - n, 1), F32)], axis=0)


def tables_kernel(ext, gate_bias, up_bias, router_t, router_d, inverse, gu_bias):
    gu_bias[:FF] = column(gate_bias[...], FF)
    gu_bias[FF:] = column(up_bias[...], FF)
    value = ext[...]
    turned = value.T
    router_t[...] = turned[2 : 2 + EXPERTS].astype(BF)
    router_d[...] = value[:, 2 : 2 + EXPERTS].astype(BF)
    gain = turned[0:1]
    inverse[...] = jnp.where(gain != 0, 1.0 / (gain * gain), 0.0)


def back_kernel(at, on, x00, x03, x01, x10, up2, down2, side2, up3, down3, weight, bias, g_out, out, chosen):
    assemble(at, (x00, x03, x01, x10, up2, down2, side2, up3, down3), g_out)
    out[:FF] = dot(weight[...], g_out[:WIDTH])
    out[FF:] = dot(jnp.broadcast_to(bias[...].astype(F32) * on[0], (8, WIDTH)).astype(BF), g_out[:WIDTH])
    chosen[...] = g_out[WIDTH : WIDTH + EXPERTS].astype(F32)


def expert_kernel(
    at, x00, x03, x01, x10, up2, down2, side2, up3, down3, chosen, back, gate_t, up_t, gate_d, up_d,
    router, router_bias, bias, inverse, mine, early, rows_out, grads_out, hidden_out, sums_out, x_out, column_out, dense,
):
    assemble(at, (x00, x03, x01, x10, up2, down2, side2, up3, down3), x_out)

    @pl.when(pl.program_id(0) == 0)
    def _():
        sums_out[...] = jnp.zeros_like(sums_out)
        column_out[...] = column(inverse[...], WIDE)

    x = x_out[...]
    xf = x.astype(F32)
    square = jnp.sum(xf * xf * column_out[...], axis=0, keepdims=True)
    scale = lax.rsqrt(square * (1.0 / WIDTH) + EPSILON)
    logits = scale * dot(router[...], x) + router_bias[...]
    gate = jnp.sum(masked_gates(logits, chosen[...]) * mine[...], axis=0, keepdims=True)
    gate_tanh = jnp.tanh((scale * dot(gate_t[...], x[:WIDTH]) + bias[:FF]) * (1.0 / 7.0))
    up_tanh = jnp.tanh((scale * dot(up_t[...], x[:WIDTH]) + bias[FF:]) * (1.0 / 7.0))
    gate_c = 7.0 * gate_tanh
    up_c = 7.0 * up_tanh
    sigma = 1.0 / (1.0 + jnp.exp(-1.702 * gate_c))
    glu = gate_c * sigma
    hidden = ((up_c + 1.0) * glu).astype(BF).astype(F32)
    down_back = back[:FF]
    gates_part = jnp.sum(hidden * down_back, axis=0, keepdims=True) + back[FF : FF + 1]
    act_grad = gate * down_back
    gate_grad = act_grad * (up_c + 1.0) * (sigma + 1.702 * glu * (1.0 - sigma)) * (1.0 - gate_tanh * gate_tanh)
    up_grad = act_grad * glu * (1.0 - up_tanh * up_tanh)
    both = jnp.concatenate([gate_grad, up_grad], axis=0).astype(BF)
    bothf = both.astype(F32)
    grads_out[...] = (scale * bothf).astype(BF)

    sums_out[...] += jnp.sum(bothf, axis=1, keepdims=True)
    high, low = split(gate)
    weighted = (gate * hidden).astype(BF)
    hidden_out[...] = jnp.concatenate([weighted.astype(F32), rows_mask(8, high, low)], axis=0).astype(BF)
    dense[:WIDTH] = (dot(gate_d[...], gate_grad.astype(BF)) + dot(up_d[...], up_grad.astype(BF))).astype(BF)
    high, low = split(gates_part)
    dense[WIDTH:] = rows_mask(WIDE - WIDTH, high, low).astype(BF)
    for r in range(TN):
        rows_out[r] = dense[pl.ds(pl.multiple_of(at[r] * COLS, COLS), COLS)]


def down_kernel(at, hidden, weight, bias, out, column_out, dense):
    @pl.when(pl.program_id(0) == 0)
    def _():
        column_out[...] = column(bias[...], WIDE)

    gate = hidden[FF : FF + 1].astype(F32) + hidden[FF + 1 : FF + 2].astype(F32)
    dense[...] = (dot(weight[...], hidden[:FF]) + column_out[...] * gate).astype(BF)
    for r in range(TN):
        out[r] = dense[pl.ds(pl.multiple_of(at[r] * COLS, COLS), COLS)]


def assemble_kernel(at, x00, x03, x01, x10, up2, down2, side2, up3, down3, early, out):
    assemble(at, (x00, x03, x01, x10, up2, down2, side2, up3, down3), out)


def finish_kernel(at, own, left, right, side, early, early2, out):
    total = own[0].astype(F32) + left[...].astype(F32) + right[...].astype(F32) + side[...].astype(F32)
    high, low = split(total[SPARE : SPARE + 1] + total[SPARE + 1 : SPARE + 2])
    tail = jnp.where(at[0] == TN - 1, rows_mask(COLS - SPARE, high, low), total[SPARE:])
    out[...] = jnp.concatenate([total[:SPARE], tail], axis=0).T.astype(BF)


def gate_weights_kernel(grads, x, early, gate_out, up_out):
    both = dot(grads[...], x[...], NT)
    gate_out[...] = both[:FF]
    up_out[...] = both[FF:]


def down_weights_kernel(hidden, g, early, weight_out, bias_out):
    both = dot(hidden[...], g[...], NT)
    weight_out[...] = both[:FF]
    bias_out[...] = jnp.broadcast_to(both[FF : FF + 1] + both[FF + 1 : FF + 2], bias_out.shape)


def combine_kernel(at, got, place, out):
    rows = got[...].reshape(SLOTS, COLS)
    value = dot(rows, place[...], TNN)
    gates = rows[:, SPARE : SPARE + 1].astype(F32) + rows[:, SPARE + 1 : SPARE + 2].astype(F32)
    gates = jnp.sum((gates * place[...].astype(F32)).reshape(EXPERTS, CAP, ROWS), axis=1)
    tail = jnp.concatenate(list(split(gates)) + [jnp.zeros((COLS - SPARE - 2 * EXPERTS, ROWS), F32)], axis=0)
    tail = jnp.where(at[0] == TN - 1, tail, value[SPARE:])
    value = jnp.concatenate([value[:SPARE], tail], axis=0).astype(BF)
    for t in range(TN):
        out[t] = value


def state_kernel(
    back, hidden, cotangent, ext, scale, gates, router_d, w, probs, sinkp, q, rim, own, cos, sin,
    heads_out, state_out, part_out, q_out, rim_out, own_out, sink_out, packed, small, dense, low,
):
    gain = ext[:WIDTH, 0:1]
    normed = hidden[:WIDTH].astype(F32) * scale[...]
    gate_grads = back[WIDTH : WIDTH + EXPERTS].astype(F32) + back[WIDTH + EXPERTS : WIDTH + 2 * EXPERTS].astype(F32)
    logit_grad = gates[...] * (gate_grads - jnp.sum(gates[...] * gate_grads, axis=0, keepdims=True))
    logit_low = jnp.concatenate([logit_grad, jnp.zeros((ROWS - EXPERTS, ROWS), F32)], axis=0).astype(BF)
    second_grad = back[:WIDTH].astype(F32) + dot(router_d[:WIDTH], logit_low[:EXPERTS])
    vectors = dot((normed * gain).astype(BF), logit_low, NT)
    lane = lax.broadcasted_iota(jnp.int32, (WIDTH, ROWS), 1)
    vectors = jnp.where(lane == EXPERTS, jnp.sum(second_grad * normed, axis=1, keepdims=True), vectors)
    scaled = second_grad * gain
    mean = jnp.sum(scaled * normed, axis=0, keepdims=True) * (1.0 / WIDTH)
    state = cotangent[...].astype(F32) + scale[...] * (scaled - normed * mean)
    state_out[...] = state
    packed[...] = jnp.zeros_like(packed)
    for k in range(DP):
        packed[k * CPAD : k * CPAD + CHUNK] = state_out[k * CHUNK : (k + 1) * CHUNK]
    vectors = jnp.where(lane == EXPERTS + 1, jnp.sum(state, axis=1, keepdims=True), vectors)
    dense[...] = vectors
    small[...] = jnp.zeros_like(small)
    logit_sum = dot(jnp.ones((8, ROWS), BF), logit_low, NT)
    forward = heads_out[...]
    for k in range(DP):
        small[:CHUNK] = dense[k * CHUNK : (k + 1) * CHUNK]
        small[CHUNK : CHUNK + 1] = logit_sum[0:1]
        low[k] = packed[k * CPAD : (k + 1) * CPAD].astype(BF)
        part_out[k, :, :Q] = dot(low[k], forward, NT).astype(BF)
        part_out[k, :, Q:] = small[...].astype(BF)
    heads = jnp.zeros((ROWS, Q), F32)
    for k in range(DP):
        heads += dot(low[k], w[k, :, :Q], TNN)
    heads = heads.T.astype(BF)
    heads = jnp.concatenate([heads[h * HEAD_DIM : (h + 1) * HEAD_DIM] for h in range(HEADS)], axis=1)
    keys = jnp.concatenate([rim[:HEAD_DIM], own[:HEAD_DIM]], axis=1)
    values = jnp.concatenate([rim[HEAD_DIM:], own[HEAD_DIM:]], axis=1).astype(F32).T.astype(BF)
    prob = probs[...]
    prob_grad = dot(values, heads)
    delta = jnp.sum(prob * prob_grad, axis=0, keepdims=True)
    score = (prob * (prob_grad - delta)).astype(BF)
    sink = -(sinkp[...] * delta)
    for h in range(HEADS):
        sink_out[h : h + 1] = sink[:, h * ROWS : (h + 1) * ROWS]
    query = 0.125 * dot(keys, score)
    c, s = cos[...], -sin[...]
    for h in range(HEADS):
        lanes = slice(h * ROWS, (h + 1) * ROWS)
        a, b = rotary(query[:HALF, lanes], query[HALF:, lanes], c, s)
        q_out[h * HEAD_DIM : h * HEAD_DIM + HALF] = a.astype(BF)
        q_out[h * HEAD_DIM + HALF : (h + 1) * HEAD_DIM] = b.astype(BF)
    key_grad = 0.125 * dot(q[...], score, NT)
    value_grad = dot(heads, prob.astype(BF), NT)
    rim_out[:HEAD_DIM] = key_grad[:, :WINDOW].astype(BF)
    rim_out[HEAD_DIM:] = value_grad[:, :WINDOW].astype(BF)
    own_out[:HEAD_DIM] = key_grad[:, WINDOW:]
    own_out[HEAD_DIM:] = value_grad[:, WINDOW:]


def first_kernel(idx, q, own, rim, sink, cos, sin, wa, wb, lin_out, part_out, pieces, dense):
    kv = own[...] + rim[...].astype(F32)
    a, b = rotary(kv[:HALF], kv[HALF:HEAD_DIM], cos[...], -sin[...])
    high, low = split(sink[...])
    lin_out[:Q] = q[...]
    lin_out[Q : Q + HALF] = a.astype(BF)
    lin_out[Q + HALF : Q + HEAD_DIM] = b.astype(BF)
    lin_out[Q + HEAD_DIM : QKV] = kv[HEAD_DIM:].astype(BF)
    lin_out[QKV:] = jnp.concatenate([high, low], axis=0).astype(BF)
    lin = lin_out[:QKV]
    for k in range(8):
        pieces[idx[k]] = dot(wa[k], lin)
        pieces[idx[8 + k]] = dot(wb[k], lin)
    dense[WIDTH:] = jnp.zeros((WIDE - WIDTH, ROWS), F32)
    for k in range(DP):
        dense[k * CHUNK : (k + 1) * CHUNK] = pieces[k, :CHUNK]
    part_out[...] = dense[...].astype(BF).reshape(TN, COLS, ROWS)


def first_slice_kernel(at, got, residual, scale, out):
    total = got[0].astype(F32)
    for t in range(1, TN):
        total += got[t].astype(F32)
    mine = pl.ds(pl.multiple_of(at[0] * COLS, COLS), COLS)
    normed = residual[mine].astype(F32) * scale[...]
    high, low = split(jnp.sum(total * normed, axis=0, keepdims=True))
    for t in range(TN):
        out[t, :COLS] = total.astype(BF)
        out[t, COLS:] = rows_mask(16, high, low).astype(BF)


def mix_kernel(mixed, place, gains, out):
    mixture = dot(mixed[...].reshape(SLOTS, COLS), place[...], TNN).astype(BF)
    for t in range(TN):
        out[t, :COLS] = mixture
        out[t, COLS:] = gains[...]


def input_kernel(got, state, residual, scale, out):
    mean = jnp.zeros((1, ROWS), F32)
    for t in range(TN):
        mean += got[t, COLS : COLS + 1].astype(F32) + got[t, COLS + 1 : COLS + 2].astype(F32)
    mean = mean * (1.0 / WIDTH)
    for t in range(TN):
        n = COLS if t < TN - 1 else SPARE
        here = slice(t * COLS, t * COLS + n)
        normed = residual[here].astype(F32) * scale[...]
        out[here] = state[here] + scale[...] * (got[t, :n].astype(F32) - normed * mean)


def block_kernel(got, hidden, out, gain_out):
    gains = jnp.zeros((32, ROWS), F32)
    for t in range(TN):
        n = COLS if t < TN - 1 else SPARE
        here = slice(t * COLS, t * COLS + n)
        out[here] = hidden[here].astype(F32) + got[t, :n].astype(F32)
        gains += got[t, COLS:].astype(F32)
    gain_out[...] = gains


def qkv_weights_kernel(idx, chunk, la, lb, own, gain, out, bias_out, sink_out, gain_out):
    acc = jnp.zeros((CPAD, QKV), F32)
    bias = jnp.zeros((QKV, ROWS), F32)
    sinks = jnp.zeros((HEADS, ROWS), F32)
    for k in range(8):
        for j, ref in ((k, la), (8 + k, lb)):
            acc += dot(chunk[idx[j]], ref[k, :QKV], NT)
            bias += ref[k, :QKV].astype(F32)
            tail = ref[k, QKV:].astype(F32)
            sinks += tail[:HEADS] + tail[HEADS:]
    acc = acc[:CHUNK]
    out[...] = acc * gain[...]
    bias_out[...] = jnp.sum(bias, axis=1, keepdims=True)
    sink_out[...] = jnp.sum(sinks, axis=1, keepdims=True)
    gains = jnp.broadcast_to(jnp.sum(acc * own[...].astype(F32), axis=1, keepdims=True), (CHUNK, ROWS)).T[0:1]
    gains = jnp.concatenate([gains, jnp.zeros((1, 2 * ROWS - CHUNK), F32)], axis=1)
    high, low = split(gains)
    first, second = rows_mask(16, high, low)[:, :ROWS], rows_mask(16, high, low)[:, ROWS:]
    gain_out[...] = jnp.concatenate([first, second], axis=0).astype(BF)


def after(value, *first):
    return pl.pallas_call(
        lambda *refs: None,
        out_shape=shape(value.shape, value.dtype),
        in_specs=[ANY] * (1 + len(first)),
        out_specs=ANY,
        input_output_aliases={0: 0},
        name="after",
    )(held(value), *map(held, first))


def exchange(value, axis):
    return lax.all_to_all(value, axis, split_axis=0, concat_axis=0, tiled=True)


def spread(value, axis):
    return exchange(jnp.broadcast_to(value[None], (lax.axis_size(axis),) + value.shape), axis)


def copies(value, count):
    return jnp.broadcast_to(value[None], (count,) + value.shape)


def along_tensor(value, dz, dy):
    pairs = [(z * 4 + y, ((z + dz) % 2) * 4 + (y + dy) % 4) for z in range(2) for y in range(4)]
    return lax.ppermute(value, "tensor", pairs)


def along_dp(value, dx, dh, dc):
    pairs = [
        (x * 4 + h * 2 + c, ((x + dx) % 4) * 4 + ((h + dh) % 2) * 2 + (c + dc) % 2)
        for x in range(4)
        for h in range(2)
        for c in range(2)
    ]
    return lax.ppermute(value, "dp", pairs)


GATHER_FROM = ((0, 0), (0, 1), (3, 0), (1, 0), (2, 0), (3, 1), (1, 1), (2, 1))


def gather_dp(value, late):
    far = along_dp(value, 0, 1, 0)
    near = [along_dp(value, dx, 0, 0) for dx in (1, 3, 2)]
    more = [along_dp(far, dx, 0, 0) for dx in (1, 3, 2)]
    pieces = [value, far] + near + more
    this_core = call(stack_kernel, shape((8,) + value.shape, BF), pieces, us=2, after=late, name="stack")
    return this_core, along_dp(this_core, 0, 0, 1)


def gather_order(me):
    x, h, c = me // 4, (me // 2) % 2, me % 2
    return jnp.stack(
        [
            ((x + dx) % 4) * 4 + ((h + dh) % 2) * 2 + (c + dc) % 2
            for dc in range(2)
            for dx, dh in GATHER_FROM
        ]
    )


def gather_tensor(value, middle, early):
    n = COLS // 2
    x03 = along_tensor(value, 0, 1)
    x01 = along_tensor(value, 0, 3)
    x10 = along_tensor(value, 1, 0)

    def pair(a, b):
        return after(jnp.stack([a, b]), *middle) if middle else jnp.stack([a, b])

    up2 = along_tensor(pair(x03[:n], x10[:n]), 0, 1)
    down2 = along_tensor(pair(x01[n:], x10[n:]), 0, 3)
    side2 = along_tensor(pair(x03[n:], x01[:n]), 1, 0)
    up3 = along_tensor(after(up2[1], early), 0, 1)
    down3 = along_tensor(after(down2[1], early), 0, 3)
    return value, x03, x01, x10, up2, down2, side2, up3, down3


def tensor_order(me):
    z, y = me // 4, me % 4
    return jnp.stack([((z + r // 4) % 2) * 4 + (y + r % 4) % 4 for r in range(TN)])


def scatter_tensor(rows, steps=((), (), ())):
    n = COLS // 2

    def add(*values):
        total = values[0].astype(F32)
        for v in values[1:]:
            total = total + v.astype(F32)
        return total.astype(BF)

    sent = []

    def send(step, value, dz, dy):
        sent.append(after(value, *steps[step]) if steps[step] else value)
        return along_tensor(sent[-1], dz, dy)

    left = send(0, rows[6, :n], 0, 3)
    right = send(0, rows[6, n:], 0, 1)
    left2 = send(1, jnp.stack([add(rows[7, :n], left), rows[2, :n]]), 0, 3)
    right2 = send(1, jnp.stack([add(rows[5, n:], right), rows[2, n:]]), 0, 1)
    side2 = send(1, jnp.stack([rows[7, n:], rows[5, :n]]), 1, 0)
    join = jnp.concatenate
    left3 = send(2, add(rows[3], join([left2[1], side2[0]])), 0, 3)
    right3 = send(2, add(rows[1], join([side2[1], right2[1]])), 0, 1)
    side3 = send(2, add(rows[4], join([left2[0], right2[0]])), 1, 0)
    return (left3, right3, side3), sent[-3:]


def segments(lengths, token_index):
    seq_ends = jnp.cumsum(lengths)
    seq_starts = seq_ends - lengths
    segment = jnp.sum((token_index[:, None] >= seq_ends[None, :]).astype(jnp.int32), axis=1)
    member = segment[:, None] == jnp.arange(lengths.shape[0], dtype=jnp.int32)[None, :]
    position = token_index - jnp.sum(jnp.where(member, seq_starts[None, :], 0), axis=1)
    return (segment, position)


def pad_rows(a, rows):
    return jnp.pad(a, ((0, rows - a.shape[0]),) + ((0, 0),) * (a.ndim - 1))


def fold(chunks):
    return jnp.concatenate([chunks[:, 64 * i : 64 * i + 64] for i in range(3)], axis=2)


def unfold(rows):
    return jnp.concatenate([rows[:, :, 128 * i : 128 * i + 128] for i in range(3)], axis=1)


def local(
    residual,
    attn_gain,
    query_weight,
    query_bias,
    key_matrix,
    key_offset_bias,
    value_matrix,
    value_offset_bias,
    attention_sink_logits,
    out_weight,
    out_bias,
    mlp_gain,
    router_weight,
    router_bias,
    gate_weight,
    gate_bias,
    up_weight,
    up_bias,
    down_weight,
    down_bias,
    routes,
    lengths,
    cotangent,
):
    me_dp = lax.axis_index("dp")
    me_t = lax.axis_index("tensor")
    at = me_t[None].astype(jnp.int32)
    order_dp = gather_order(me_dp).astype(jnp.int32)
    order_t = tensor_order(me_t).astype(jnp.int32)

    gain_own = attn_gain.astype(F32)[:, None]
    own_qkv = jnp.concatenate([query_weight, key_matrix, value_matrix], axis=1)
    residual_t = residual.T
    inputs = residual_t.astype(F32)
    scale_one = lax.rsqrt(jnp.mean(inputs * inputs, axis=0, keepdims=True) + EPSILON)
    normed = (inputs * scale_one).astype(BF)
    normed_chunks = jnp.pad(normed.reshape(DP, CHUNK, ROWS), ((0, 0), (0, CPAD - CHUNK), (0, 0)))
    normed_rim = lax.ppermute(normed_chunks, "dp", [(i, i + 1) for i in range(DP - 1)])
    small = jnp.concatenate(
        [mlp_gain[:, None], out_bias[:, None], router_weight, jnp.zeros((CHUNK, 110), BF)], axis=1
    )
    out_all = lax.all_gather(pad_rows(jnp.concatenate([out_weight, small], axis=1), CPAD), "dp")
    qkv_a, qkv_b = gather_dp(pad_rows((own_qkv.astype(F32) * gain_own).astype(BF), CPAD), ())

    expert_ids = jnp.arange(EXPERTS, dtype=jnp.int32)
    member = jnp.any(routes.T[None, :, :] == expert_ids[:, None, None], axis=1)
    above = (jnp.arange(ROWS)[:, None] < jnp.arange(ROWS)[None, :]).astype(BF)
    rank = dot(member.astype(BF), above).astype(jnp.int32)
    place = (
        (rank[:, None, :] == jnp.arange(CAP, dtype=jnp.int32)[None, :, None]) & member[:, None, :]
    ).astype(BF).reshape(SLOTS, ROWS)
    member = member.astype(F32)

    cotangent_t = cotangent.T
    grad_ext = pad_rows(jnp.concatenate([cotangent_t, member.astype(BF)], axis=0), WIDE)
    grad_cols = lax.dynamic_slice_in_dim(grad_ext, me_t * COLS, COLS, 0)
    grad_slots = dot(place, grad_cols, NT).astype(BF).reshape(EXPERTS, CAP, COLS)
    grad_cols_t = call(
        turn_kernel, shape((COLS, SLOTS), BF), (exchange(grad_slots, "dp"),), us=2, name="turn_grad"
    )

    gate_t, up_t, down = gate_weight[0].T, up_weight[0].T, down_weight[0]
    gate_d, up_d, down_d = gate_weight[0], up_weight[0], jnp.pad(down.T, ((0, WIDE - WIDTH), (0, 0)))
    bias_on = (me_t == 0).astype(F32)[None]
    mine = (expert_ids == me_dp).astype(F32)[:, None]
    bias_router = router_bias.astype(F32)[:, None]

    starting_row = me_dp * ROWS
    token_index = starting_row + jnp.arange(ROWS, dtype=jnp.int32)
    segment, position = segments(lengths, token_index)
    key_index = starting_row - WINDOW + jnp.arange(ROWS + WINDOW, dtype=jnp.int32)
    key_segment, unused = segments(lengths, key_index)
    offset = token_index[None, :] - key_index[:, None]
    mask = (
        (segment[None, :] == key_segment[:, None])
        & (offset >= 0)
        & (offset < WINDOW)
        & (key_index[:, None] >= 0)
    ).astype(F32)
    frequency = ROPE_BASE ** (-2.0 * jnp.arange(HALF, dtype=F32) / HEAD_DIM)
    angle = position.astype(F32)[None, :] * frequency[:, None]
    cos, sin = jnp.cos(angle), jnp.sin(angle)
    unused, rim_position = segments(lengths, key_index[:WINDOW])
    rim_angle = rim_position.astype(F32)[None, :] * frequency[:, None]
    cos_rim, sin_rim = jnp.cos(rim_angle), jnp.sin(rim_angle)
    sink = jnp.repeat(attention_sink_logits.astype(F32), ROWS)[None]
    bias = jnp.concatenate([query_bias, key_offset_bias, value_offset_bias]).astype(F32)[None]
    ready = (mine, bias_router, mask, sink, grad_cols_t)
    query, own_kv, rim_kv = call(
        qkv_kernel,
        (shape((HEAD_DIM, CAT), BF), shape((2 * HEAD_DIM, ROWS), BF), shape((2 * HEAD_DIM, ROWS), BF)),
        (
            order_dp, qkv_a, qkv_b, normed_chunks, normed_rim, bias,
            cos, sin, cos_rim, sin_rim,
        ),
        smem=1,
        after=ready,
        mib=40, name="qkv",
    )
    probs, sink_probs, heads_out, branch, ext = call(
        attention_kernel,
        (
            shape((2 * WINDOW, CAT), F32),
            shape((1, CAT), F32),
            shape((Q, ROWS), BF),
            shape((WIDE, ROWS), BF),
            shape((WIDE, ROWS), F32),
        ),
        (query, rim_kv, own_kv, mask, sink, out_all),
        scratch=[pltpu.VMEM((WIDE, ROWS), F32)],
        mib=40, name="attention",
    )
    branch = exchange(branch.reshape(TN, COLS, ROWS), "tensor")

    grad_pieces = gather_tensor(after(grad_cols_t, heads_out), (), heads_out)
    tile = 256
    steps = SLOTS // tile
    def whole(a):
        return pl.BlockSpec(a.shape, lambda i, n=len(a.shape): (0,) * n)

    def lanes(a):
        n = len(a.shape)
        return pl.BlockSpec(a.shape[:-1] + (tile,), lambda i: (0,) * (n - 1) + (i,))

    back_outs = (shape((WIDE, SLOTS), BF), shape((FF + 8, SLOTS), F32), shape((EXPERTS, SLOTS), F32))
    grad_rows, down_back, chosen = pl.pallas_call(
        back_kernel,
        grid=(steps,),
        in_specs=[SMEM, SMEM] + [lanes(a) for a in grad_pieces] + [whole(down), whole(down_bias)],
        out_specs=[lanes(a) for a in back_outs],
        out_shape=back_outs,
        compiler_params=params(24),
        cost_estimate=cost(8),
        name="back",
    )(order_t, bias_on, *map(held, grad_pieces + (down, down_bias)))
    hidden_cols, out_rows = call(
        slice_kernel,
        (shape((TN, COLS, ROWS), BF), shape((EXPERTS, CAP, COLS), BF)),
        (at, branch, pad_rows(residual_t, WIDE), ext, place),
        smem=1,
        name="slice",
    )
    expert_cols = call(
        turn_kernel,
        shape((COLS, SLOTS), BF),
        (exchange(out_rows, "dp"),),
        after=(gate_d, up_d, down_d),
        us=2,
        name="turn",
    )
    router_t, router_d, inverse, gu_bias = call(
        tables_kernel,
        (
            shape((EXPERTS, WIDE), BF),
            shape((WIDE, EXPERTS), BF),
            shape((1, WIDE), F32),
            shape((2 * FF, 1), F32),
        ),
        (ext, gate_bias, up_bias),
        after=(expert_cols,),
        name="tables",
    )

    hidden = exchange(after(hidden_cols, expert_cols), "tensor").reshape(WIDE, ROWS)
    scale_two, gates = call(
        gates_kernel,
        (shape((1, ROWS), F32), shape((EXPERTS, ROWS), F32)),
        (hidden, ext, router_t, bias_router, member),
        name="gates",
    )
    pieces = gather_tensor(expert_cols, (), gates)

    early = (grad_rows,)
    tiled = pieces + (chosen, down_back)
    full = (gate_t, up_t, gate_d, up_d, router_t, bias_router, gu_bias, inverse, mine)
    outs = (
        shape((TN, COLS, SLOTS), BF),
        shape((2 * FF, SLOTS), BF),
        shape((FF + 8, SLOTS), BF),
        shape((2 * FF, 1), F32),
    )
    rows_back, expert_grads, expert_hidden, bias_sums = pl.pallas_call(
        expert_kernel,
        grid=(steps,),
        in_specs=[SMEM] + [lanes(a) for a in tiled] + [whole(a) for a in full] + [ANY] * len(early),
        out_specs=[lanes(a) for a in outs[:3]] + [whole(outs[3])],
        out_shape=outs,
        scratch_shapes=[pltpu.VMEM((WIDE, tile), BF), pltpu.VMEM((WIDE, 1), F32), pltpu.VMEM((WIDE, tile), BF)],
        compiler_params=params(44),
        cost_estimate=cost(20),
        name="expert",
    )(order_t, *map(held, tiled + full + early))
    mixed_rows = pl.pallas_call(
        down_kernel,
        grid=(steps,),
        in_specs=[SMEM, lanes(outs[2]), whole(down_d), whole(down_bias)],
        out_specs=lanes(outs[0]),
        out_shape=outs[0],
        scratch_shapes=[pltpu.VMEM((WIDE, 1), F32), pltpu.VMEM((WIDE, tile), BF)],
        compiler_params=params(24),
        cost_estimate=cost(6),
        name="down",
    )(order_t, held(expert_hidden), held(down_d), held(down_bias * bias_on.astype(BF)))
    expert_in = pl.pallas_call(
        assemble_kernel,
        grid=(steps,),
        in_specs=[SMEM] + [lanes(a) for a in pieces] + [ANY],
        out_specs=pl.BlockSpec((WIDE, tile), lambda i: (0, i)),
        out_shape=shape((WIDE, SLOTS), BF),
        compiler_params=params(16),
        cost_estimate=cost(5),
        name="assemble",
    )(order_t, *map(held, pieces), held(expert_hidden))
    chunk_got = exchange(after(fold(normed_chunks), expert_hidden), "dp")
    first_chunk = unfold(chunk_got)

    (left, right, side), unused = scatter_tensor(rows_back, ((), (), (chunk_got,)))
    square = (COLS, SLOTS)

    def finish(rows, left, right, side, *early):
        return pl.pallas_call(
            finish_kernel,
            grid=(1,),
            in_specs=[SMEM, pl.BlockSpec((1,) + square, lambda i: (0, 0, 0))]
            + [pl.BlockSpec(square, lambda i: (0, 0))] * 3
            + [ANY] * 2,
            out_specs=pl.BlockSpec((SLOTS, COLS), lambda i: (0, 0)),
            out_shape=shape((SLOTS, COLS), BF),
            compiler_params=params(10),
            cost_estimate=cost(2),
            name="finish",
        )(at, *map(held, (rows, left, right, side) + early)).reshape(EXPERTS, CAP, COLS)

    back_cols = finish(rows_back, left, right, side, mixed_rows, mixed_rows)
    back_got = exchange(back_cols, "dp")
    back_tokens = call(
        combine_kernel, shape((TN, COLS, ROWS), BF), (at, back_got, place), smem=1,
        after=(expert_in,), name="combine",
    )
    back_all = exchange(back_tokens, "tensor").reshape(WIDE, ROWS)

    (mixed_left, mixed_right, mixed_side), mixed_sent = scatter_tensor(
        mixed_rows, ((left, right, side), (), (back_all,))
    )

    state, out_parts, q_grad, rim_grad, kv_grad, sink_grad = call(
        state_kernel,
        (
            shape((WIDTH, ROWS), F32),
            shape((DP, CPAD, Q + ROWS), BF),
            shape((Q, ROWS), BF),
            shape((2 * HEAD_DIM, WINDOW), BF),
            shape((2 * HEAD_DIM, ROWS), F32),
            shape((HEADS, ROWS), F32),
        ),
        (
            back_all, hidden, cotangent_t, ext, scale_two, gates, router_d, out_all, probs,
            sink_probs, query, rim_kv, own_kv, cos, sin, heads_out,
        ),
        scratch=[
            pltpu.VMEM((DP * CPAD, ROWS), F32),
            pltpu.VMEM((CPAD, ROWS), F32),
            pltpu.VMEM((WIDTH, ROWS), F32),
            pltpu.VMEM((DP, CPAD, ROWS), BF),
        ],
        mib=56, name="state",
    )
    rim_grad = lax.ppermute(rim_grad, "dp", [(i + 1, i) for i in range(DP - 1)])
    lin_grad, first_part = call(
        first_kernel,
        (shape((QKV + 16, ROWS), BF), shape((TN, COLS, ROWS), BF)),
        (order_dp, q_grad, kv_grad, rim_grad, sink_grad, cos, sin, qkv_a, qkv_b),
        smem=1,
        scratch=[pltpu.VMEM((DP, CPAD, ROWS), F32), pltpu.VMEM((WIDE, ROWS), F32)],
        after=tuple(mixed_sent),
        mib=40, name="first",
    )
    out_sums = lax.psum_scatter(out_parts, "dp", scatter_dimension=0)
    first_got = exchange(first_part, "tensor")

    def block(rows):
        return pl.BlockSpec((rows, COLS), lambda j: (0, j))

    grad_gate, grad_up = pl.pallas_call(
        gate_weights_kernel,
        grid=(TN,),
        in_specs=[
            pl.BlockSpec((2 * FF, SLOTS), lambda j: (0, 0)),
            pl.BlockSpec((COLS, SLOTS), lambda j: (j, 0)),
            ANY,
        ],
        out_specs=[block(FF), block(FF)],
        out_shape=(shape((FF, WIDTH), F32), shape((FF, WIDTH), F32)),
        compiler_params=params(16),
        cost_estimate=cost(12),
        name="gate_weights",
    )(held(expert_grads), held(expert_in), held(first_part))
    mixed_cols = finish(mixed_rows, mixed_left, mixed_right, mixed_side, back_all, grad_gate)
    first_cols = call(
        first_slice_kernel,
        shape((TN, COLS + 16, ROWS), BF),
        (at, first_got, pad_rows(residual_t, WIDE), scale_one),
        smem=1,
        name="first_slice",
    )
    lin_a, lin_b = gather_dp(after(lin_grad, first_cols, mixed_cols), ())
    grad_qkv, grad_bias, grad_sinks, gain_rows = call(
        qkv_weights_kernel,
        (shape((CHUNK, QKV), F32), shape((QKV, 1), F32), shape((HEADS, 1), F32), shape((32, ROWS), BF)),
        (order_dp, first_chunk, lin_a, lin_b, own_qkv, gain_own),
        smem=1,
        name="qkv_weights",
    )
    grad_down, grad_down_bias = pl.pallas_call(
        down_weights_kernel,
        grid=(TN,),
        in_specs=[
            pl.BlockSpec((FF + 8, SLOTS), lambda j: (0, 0)),
            pl.BlockSpec((COLS, SLOTS), lambda j: (j, 0)),
            ANY,
        ],
        out_specs=[block(FF), block(8)],
        out_shape=(shape((FF, WIDTH), F32), shape((8, WIDTH), F32)),
        compiler_params=params(16),
        cost_estimate=cost(9),
        name="down_weights",
    )(held(expert_hidden), held(grad_rows), held(first_got))

    first_all = exchange(first_cols, "tensor")
    mixed_got = exchange(after(mixed_cols, first_all), "dp")
    mixed_out = call(
        mix_kernel,
        shape((TN, COLS + 32, ROWS), BF),
        (mixed_got, place, gain_rows),
        after=(grad_down,),
        name="mix",
    )
    grad_input = call(
        input_kernel,
        shape((WIDTH, ROWS), F32),
        (first_all, state, residual_t, scale_one),
        name="input",
    )
    block_out, gains = call(
        block_kernel,
        (shape((WIDTH, ROWS), F32), shape((32, ROWS), F32)),
        (exchange(mixed_out, "tensor"), hidden),
        name="block",
    )
    gains = jnp.concatenate([gains[0] + gains[1], gains[16] + gains[17]])
    out_sums = out_sums[:CHUNK + 1].astype(F32)

    return (
        block_out.T,
        grad_input.T,
        gains[:CHUNK],
        grad_qkv[:, :Q],
        grad_bias[:Q, 0],
        grad_qkv[:, Q : Q + HEAD_DIM],
        grad_bias[Q : Q + HEAD_DIM, 0],
        grad_qkv[:, Q + HEAD_DIM :],
        grad_bias[Q + HEAD_DIM :, 0],
        grad_sinks[:, 0],
        out_sums[:CHUNK, :Q],
        out_sums[:CHUNK, Q + EXPERTS + 1],
        out_sums[:CHUNK, Q + EXPERTS],
        out_sums[:CHUNK, Q : Q + EXPERTS],
        out_sums[CHUNK, Q : Q + EXPERTS],
        grad_gate.T[None],
        bias_sums[None, :FF, 0],
        grad_up.T[None],
        bias_sums[None, FF:, 0],
        grad_down[None],
        grad_down_bias[:1],
    )


def solution(mesh):
    return jax.shard_map(
        local,
        mesh=mesh,
        in_specs=(
            P("dp", None),
            P("dp"),
            P("dp", "tensor"),
            P("tensor"),
            P("dp", "tensor"),
            P("tensor"),
            P("dp", "tensor"),
            P("tensor"),
            P("tensor"),
            P("dp", "tensor"),
            P("dp"),
            P("dp"),
            P("dp", None),
            P(),
            P("dp", None, "tensor"),
            P("dp", "tensor"),
            P("dp", None, "tensor"),
            P("dp", "tensor"),
            P("dp", "tensor", None),
            P("dp", None),
            P("dp", None),
            P(),
            P("dp", None),
        ),
        out_specs=(
            P("dp", None),
            P("dp", None),
            P("dp"),
            P("dp", "tensor"),
            P("tensor"),
            P("dp", "tensor"),
            P("tensor"),
            P("dp", "tensor"),
            P("tensor"),
            P("tensor"),
            P("dp", "tensor"),
            P("dp"),
            P("dp"),
            P("dp", None),
            P(),
            P("dp", None, "tensor"),
            P("dp", "tensor"),
            P("dp", None, "tensor"),
            P("dp", "tensor"),
            P("dp", "tensor", None),
            P("dp", None),
        ),
        check_vma=False,
    )
```

```python
import functools

import jax
import jax.numpy as jnp
from jax import lax
from jax.experimental import pallas as pl
from jax.experimental.pallas import tpu as pltpu
from jax.sharding import PartitionSpec as P

HEAD_DIM = 64
HALF = HEAD_DIM // 2
WINDOW = 128
EPSILON = 1e-05
ROPE_BASE = 150000.0
MASKED = -1000000000.0
BF = jnp.bfloat16
F32 = jnp.float32

ROWS = 128
WIDTH = 2880
EXPERTS = 16
CAP = 64
SLOTS = EXPERTS * CAP
DP = 16
TN = 8
CHUNK = WIDTH // DP
CPAD = 192
COLS = 384
WIDE = TN * COLS
SPARE = WIDTH - (TN - 1) * COLS
FF = 360
HEADS = 8
Q = HEADS * HEAD_DIM
QKV = Q + 2 * HEAD_DIM
CAT = HEADS * ROWS

VMEM = pl.BlockSpec(memory_space=pltpu.VMEM)
SMEM = pl.BlockSpec(memory_space=pltpu.SMEM)
ANY = pl.BlockSpec(memory_space=pl.ANY)
NN = ((1,), (0,))
NT = ((1,), (1,))
TNN = ((0,), (0,))


def dot(a, b, dims=NN):
    return lax.dot_general(a, b, (dims, ((), ())), preferred_element_type=F32)


def params(mib=48):
    return pltpu.CompilerParams(vmem_limit_bytes=mib << 20)


def cost(us):
    return pl.CostEstimate(flops=int(us * 1e9), bytes_accessed=int(us * 3.2e6), transcendentals=0)


def shape(dims, dtype):
    return pltpu.HBM(dims, dtype)


def held(a):
    return pltpu.with_memory_space_constraint(a, pltpu.HBM)


def call(body, outs, args, smem=0, scratch=(), after=(), us=3, mib=26, name=None):
    n = len(args)
    run = (lambda *refs: body(*refs[:n], *refs[n + len(after) :])) if after else body
    return pl.pallas_call(
        run,
        out_shape=outs,
        in_specs=[SMEM] * smem + [VMEM] * (n - smem) + [ANY] * len(after),
        out_specs=jax.tree.map(lambda _: VMEM, outs),
        scratch_shapes=list(scratch),
        compiler_params=params(mib),
        cost_estimate=cost(us),
        name=name,
    )(*args[:smem], *map(held, args[smem:]), *map(held, after))


def rows_mask(rows, first, second):
    n = first.shape[1]
    at = lax.broadcasted_iota(jnp.int32, (rows, n), 0)
    return jnp.where(at == 0, first, jnp.where(at == 1, second, 0.0))


def split(value):
    high = value.astype(BF).astype(F32)
    return high, value - high


def rotary(a, b, cos, sin):
    return a * cos - b * sin, b * cos + a * sin


def qkv_kernel(idx, wa, wb, x, x_rim, bias, cos, sin, cos_rim, sin_rim, q_out, kv_out, rim_out):
    acc = jnp.zeros((ROWS, QKV), F32)
    rim = jnp.zeros((ROWS, 2 * HEAD_DIM), F32)
    for k in range(8):
        for j, w in ((k, wa[k]), (8 + k, wb[k])):
            acc += dot(x[idx[j]], w, TNN)
            rim += dot(x_rim[idx[j]], w[:, Q:], TNN)
    lin = (acc + bias[...]).T.reshape(HEADS + 2, HEAD_DIM, ROWS)
    c, s = cos[...], sin[...]
    for h in range(HEADS):
        a, b = rotary(lin[h, :HALF], lin[h, HALF:], c, s)
        q_out[:HALF, h * ROWS : (h + 1) * ROWS] = a.astype(BF)
        q_out[HALF:, h * ROWS : (h + 1) * ROWS] = b.astype(BF)
    rim = (rim + bias[:, Q:]).T
    for out, k, v, c, s in (
        (kv_out, lin[HEADS], lin[HEADS + 1], c, s),
        (rim_out, rim[:HEAD_DIM], rim[HEAD_DIM:], cos_rim[...], sin_rim[...]),
    ):
        a, b = rotary(k[:HALF], k[HALF:], c, s)
        out[:HALF] = a.astype(BF)
        out[HALF:HEAD_DIM] = b.astype(BF)
        out[HEAD_DIM:] = v.astype(BF)


def attention_kernel(
    q, rim, own, mask, sink, w, prob_out, sinkp_out, heads_out, branch_out, ext_out, dense
):
    keys = jnp.concatenate([rim[:HEAD_DIM], own[:HEAD_DIM]], axis=1).astype(F32).T.astype(BF)
    values = jnp.concatenate([rim[HEAD_DIM:], own[HEAD_DIM:]], axis=1)
    allowed = jnp.concatenate([mask[...]] * HEADS, axis=1) > 0
    scores = jnp.where(allowed, 0.125 * dot(keys, q[...]), MASKED)
    peak = jnp.maximum(jnp.max(scores, axis=0, keepdims=True), sink[...])
    weights = jnp.exp(scores - peak)
    sink_exp = jnp.exp(sink[...] - peak)
    inverse = 1.0 / (jnp.sum(weights, axis=0, keepdims=True) + sink_exp)
    probs = weights * inverse
    prob_out[...] = probs
    sinkp_out[...] = sink_exp * inverse
    mixed = dot(values, probs.astype(BF)).astype(BF)
    for h in range(HEADS):
        heads_out[h * HEAD_DIM : (h + 1) * HEAD_DIM] = mixed[:, h * ROWS : (h + 1) * ROWS]
    heads = heads_out[...]
    dense[WIDTH:] = jnp.zeros((WIDE - WIDTH, ROWS), F32)
    ext_out[WIDTH:] = jnp.zeros((WIDE - WIDTH, ROWS), F32)
    for k in range(DP):
        dense[k * CHUNK : (k + 1) * CHUNK] = dot(w[k, :, :Q], heads)[:CHUNK]
        ext_out[k * CHUNK : (k + 1) * CHUNK] = w[k, :, Q:].astype(F32)[:CHUNK]
    branch_out[...] = dense[...].astype(BF)


def slice_kernel(at, got, residual, ext, place, hidden_out, rows_out):
    mine = pl.ds(pl.multiple_of(at[0] * COLS, COLS), COLS)
    total = residual[mine].astype(F32) + ext[mine, 1:2]
    for t in range(TN):
        total += got[t].astype(F32)
    for t in range(TN):
        hidden_out[t] = total.astype(BF)
    moved = (total * ext[mine, 0:1]).astype(BF)
    rows_out[...] = dot(place[...], moved, NT).astype(BF).reshape(rows_out.shape)


def masked_gates(logits, chosen):
    top = jnp.max(jnp.where(chosen > 0, logits, MASKED), axis=0, keepdims=True)
    weights = jnp.where(chosen > 0, jnp.exp(logits - top), 0.0)
    total = jnp.sum(weights, axis=0, keepdims=True)
    return weights / jnp.where(total > 0, total, 1.0)


def gates_kernel(hidden, ext, router, bias, member, scale_out, gates_out):
    h = hidden[...].astype(F32)[:WIDTH]
    scale = lax.rsqrt(jnp.sum(h * h, axis=0, keepdims=True) * (1.0 / WIDTH) + EPSILON)
    scale_out[...] = scale
    second = (h * scale * ext[:WIDTH, 0:1]).astype(BF)
    logits = dot(router[:, :WIDTH], second) + bias[...]
    gates_out[...] = masked_gates(logits, member[...])


def assemble(at, pieces, out):
    x00, x03, x01, x10, up2, down2, side2, up3, down3 = pieces
    half = COLS // 2

    def put(r, value, low=None):
        start = at[r] * COLS + (half if low is False else 0)
        rows = COLS if low is None else half
        out[pl.ds(pl.multiple_of(start, half), rows)] = value

    put(0, x00[...])
    put(3, x03[...])
    put(1, x01[...])
    put(4, x10[...])
    put(2, up2[0], True)
    put(7, up2[1], True)
    put(2, down2[0], False)
    put(5, down2[1], False)
    put(7, side2[0], False)
    put(5, side2[1], True)
    put(6, up3[...], True)
    put(6, down3[...], False)


def turn_kernel(got, out):
    out[...] = got[...].reshape(SLOTS, COLS).astype(F32).T.astype(BF)


def stack_kernel(*refs):
    for k, ref in enumerate(refs[:-1]):
        refs[-1][k] = ref[...]


def column(row, rows):
    n = row.shape[1]
    value = jnp.broadcast_to(row.astype(F32), (8, n)).T[:, 0:1]
    return value if n == rows else jnp.concatenate([value, jnp.zeros((rows - n, 1), F32)], axis=0)


def tables_kernel(ext, gate_bias, up_bias, router_t, router_d, inverse, gu_bias):
    gu_bias[:FF] = column(gate_bias[...], FF)
    gu_bias[FF:] = column(up_bias[...], FF)
    value = ext[...]
    turned = value.T
    router_t[...] = turned[2 : 2 + EXPERTS].astype(BF)
    router_d[...] = value[:, 2 : 2 + EXPERTS].astype(BF)
    gain = turned[0:1]
    inverse[...] = jnp.where(gain != 0, 1.0 / (gain * gain), 0.0)


def back_kernel(at, on, x00, x03, x01, x10, up2, down2, side2, up3, down3, weight, bias, g_out, out, chosen):
    assemble(at, (x00, x03, x01, x10, up2, down2, side2, up3, down3), g_out)
    out[:FF] = dot(weight[...], g_out[:WIDTH])
    out[FF:] = dot(jnp.broadcast_to(bias[...].astype(F32) * on[0], (8, WIDTH)).astype(BF), g_out[:WIDTH])
    chosen[...] = g_out[WIDTH : WIDTH + EXPERTS].astype(F32)


def expert_kernel(
    at, x00, x03, x01, x10, up2, down2, side2, up3, down3, chosen, back, gate_t, up_t, gate_d, up_d,
    router, router_bias, bias, inverse, mine, early, rows_out, grads_out, hidden_out, sums_out, x_out, column_out, dense,
):
    assemble(at, (x00, x03, x01, x10, up2, down2, side2, up3, down3), x_out)

    @pl.when(pl.program_id(0) == 0)
    def _():
        sums_out[...] = jnp.zeros_like(sums_out)
        column_out[...] = column(inverse[...], WIDE)

    x = x_out[...]
    xf = x.astype(F32)
    square = jnp.sum(xf * xf * column_out[...], axis=0, keepdims=True)
    scale = lax.rsqrt(square * (1.0 / WIDTH) + EPSILON)
    logits = scale * dot(router[...], x) + router_bias[...]
    gate = jnp.sum(masked_gates(logits, chosen[...]) * mine[...], axis=0, keepdims=True)
    gate_tanh = jnp.tanh((scale * dot(gate_t[...], x[:WIDTH]) + bias[:FF]) * (1.0 / 7.0))
    up_tanh = jnp.tanh((scale * dot(up_t[...], x[:WIDTH]) + bias[FF:]) * (1.0 / 7.0))
    gate_c = 7.0 * gate_tanh
    up_c = 7.0 * up_tanh
    sigma = 1.0 / (1.0 + jnp.exp(-1.702 * gate_c))
    glu = gate_c * sigma
    hidden = ((up_c + 1.0) * glu).astype(BF).astype(F32)
    down_back = back[:FF]
    gates_part = jnp.sum(hidden * down_back, axis=0, keepdims=True) + back[FF : FF + 1]
    act_grad = gate * down_back
    gate_grad = act_grad * (up_c + 1.0) * (sigma + 1.702 * glu * (1.0 - sigma)) * (1.0 - gate_tanh * gate_tanh)
    up_grad = act_grad * glu * (1.0 - up_tanh * up_tanh)
    both = jnp.concatenate([gate_grad, up_grad], axis=0).astype(BF)
    bothf = both.astype(F32)
    grads_out[...] = (scale * bothf).astype(BF)

    sums_out[...] += jnp.sum(bothf, axis=1, keepdims=True)
    high, low = split(gate)
    weighted = (gate * hidden).astype(BF)
    hidden_out[...] = jnp.concatenate([weighted.astype(F32), rows_mask(8, high, low)], axis=0).astype(BF)
    dense[:WIDTH] = (dot(gate_d[...], gate_grad.astype(BF)) + dot(up_d[...], up_grad.astype(BF))).astype(BF)
    high, low = split(gates_part)
    dense[WIDTH:] = rows_mask(WIDE - WIDTH, high, low).astype(BF)
    for r in range(TN):
        rows_out[r] = dense[pl.ds(pl.multiple_of(at[r] * COLS, COLS), COLS)]


def down_kernel(at, hidden, weight, bias, out, column_out, dense):
    @pl.when(pl.program_id(0) == 0)
    def _():
        column_out[...] = column(bias[...], WIDE)

    gate = hidden[FF : FF + 1].astype(F32) + hidden[FF + 1 : FF + 2].astype(F32)
    dense[...] = (dot(weight[...], hidden[:FF]) + column_out[...] * gate).astype(BF)
    for r in range(TN):
        out[r] = dense[pl.ds(pl.multiple_of(at[r] * COLS, COLS), COLS)]


def assemble_kernel(at, x00, x03, x01, x10, up2, down2, side2, up3, down3, early, out):
    assemble(at, (x00, x03, x01, x10, up2, down2, side2, up3, down3), out)


def finish_kernel(at, own, left, right, side, early, early2, out):
    total = own[0].astype(F32) + left[...].astype(F32) + right[...].astype(F32) + side[...].astype(F32)
    high, low = split(total[SPARE : SPARE + 1] + total[SPARE + 1 : SPARE + 2])
    tail = jnp.where(at[0] == TN - 1, rows_mask(COLS - SPARE, high, low), total[SPARE:])
    out[...] = jnp.concatenate([total[:SPARE], tail], axis=0).T.astype(BF)


def gate_weights_kernel(grads, x, early, gate_out, up_out):
    both = dot(grads[...], x[...], NT)
    gate_out[...] = both[:FF]
    up_out[...] = both[FF:]


def down_weights_kernel(hidden, g, early, weight_out, bias_out):
    both = dot(hidden[...], g[...], NT)
    weight_out[...] = both[:FF]
    bias_out[...] = jnp.broadcast_to(both[FF : FF + 1] + both[FF + 1 : FF + 2], bias_out.shape)


def combine_kernel(at, got, place, out):
    rows = got[...].reshape(SLOTS, COLS)
    value = dot(rows, place[...], TNN)
    gates = rows[:, SPARE : SPARE + 1].astype(F32) + rows[:, SPARE + 1 : SPARE + 2].astype(F32)
    gates = jnp.sum((gates * place[...].astype(F32)).reshape(EXPERTS, CAP, ROWS), axis=1)
    tail = jnp.concatenate(list(split(gates)) + [jnp.zeros((COLS - SPARE - 2 * EXPERTS, ROWS), F32)], axis=0)
    tail = jnp.where(at[0] == TN - 1, tail, value[SPARE:])
    value = jnp.concatenate([value[:SPARE], tail], axis=0).astype(BF)
    for t in range(TN):
        out[t] = value


def state_kernel(
    back, hidden, cotangent, ext, scale, gates, router_d, w, probs, sinkp, q, rim, own, cos, sin,
    heads_out, state_out, part_out, q_out, rim_out, own_out, sink_out, packed, small, dense, low,
):
    gain = ext[:WIDTH, 0:1]
    normed = hidden[:WIDTH].astype(F32) * scale[...]
    gate_grads = back[WIDTH : WIDTH + EXPERTS].astype(F32) + back[WIDTH + EXPERTS : WIDTH + 2 * EXPERTS].astype(F32)
    logit_grad = gates[...] * (gate_grads - jnp.sum(gates[...] * gate_grads, axis=0, keepdims=True))
    logit_low = jnp.concatenate([logit_grad, jnp.zeros((ROWS - EXPERTS, ROWS), F32)], axis=0).astype(BF)
    second_grad = back[:WIDTH].astype(F32) + dot(router_d[:WIDTH], logit_low[:EXPERTS])
    vectors = dot((normed * gain).astype(BF), logit_low, NT)
    lane = lax.broadcasted_iota(jnp.int32, (WIDTH, ROWS), 1)
    vectors = jnp.where(lane == EXPERTS, jnp.sum(second_grad * normed, axis=1, keepdims=True), vectors)
    scaled = second_grad * gain
    mean = jnp.sum(scaled * normed, axis=0, keepdims=True) * (1.0 / WIDTH)
    state = cotangent[...].astype(F32) + scale[...] * (scaled - normed * mean)
    state_out[...] = state
    packed[...] = jnp.zeros_like(packed)
    for k in range(DP):
        packed[k * CPAD : k * CPAD + CHUNK] = state_out[k * CHUNK : (k + 1) * CHUNK]
    vectors = jnp.where(lane == EXPERTS + 1, jnp.sum(state, axis=1, keepdims=True), vectors)
    dense[...] = vectors
    small[...] = jnp.zeros_like(small)
    logit_sum = dot(jnp.ones((8, ROWS), BF), logit_low, NT)
    forward = heads_out[...]
    for k in range(DP):
        small[:CHUNK] = dense[k * CHUNK : (k + 1) * CHUNK]
        small[CHUNK : CHUNK + 1] = logit_sum[0:1]
        low[k] = packed[k * CPAD : (k + 1) * CPAD].astype(BF)
        part_out[k, :, :Q] = dot(low[k], forward, NT).astype(BF)
        part_out[k, :, Q:] = small[...].astype(BF)
    heads = jnp.zeros((ROWS, Q), F32)
    for k in range(DP):
        heads += dot(low[k], w[k, :, :Q], TNN)
    heads = heads.T.astype(BF)
    heads = jnp.concatenate([heads[h * HEAD_DIM : (h + 1) * HEAD_DIM] for h in range(HEADS)], axis=1)
    keys = jnp.concatenate([rim[:HEAD_DIM], own[:HEAD_DIM]], axis=1)
    values = jnp.concatenate([rim[HEAD_DIM:], own[HEAD_DIM:]], axis=1).astype(F32).T.astype(BF)
    prob = probs[...]
    prob_grad = dot(values, heads)
    delta = jnp.sum(prob * prob_grad, axis=0, keepdims=True)
    score = (prob * (prob_grad - delta)).astype(BF)
    sink = -(sinkp[...] * delta)
    for h in range(HEADS):
        sink_out[h : h + 1] = sink[:, h * ROWS : (h + 1) * ROWS]
    query = 0.125 * dot(keys, score)
    c, s = cos[...], -sin[...]
    for h in range(HEADS):
        lanes = slice(h * ROWS, (h + 1) * ROWS)
        a, b = rotary(query[:HALF, lanes], query[HALF:, lanes], c, s)
        q_out[h * HEAD_DIM : h * HEAD_DIM + HALF] = a.astype(BF)
        q_out[h * HEAD_DIM + HALF : (h + 1) * HEAD_DIM] = b.astype(BF)
    key_grad = 0.125 * dot(q[...], score, NT)
    value_grad = dot(heads, prob.astype(BF), NT)
    rim_out[:HEAD_DIM] = key_grad[:, :WINDOW].astype(BF)
    rim_out[HEAD_DIM:] = value_grad[:, :WINDOW].astype(BF)
    own_out[:HEAD_DIM] = key_grad[:, WINDOW:]
    own_out[HEAD_DIM:] = value_grad[:, WINDOW:]


def first_kernel(idx, q, own, rim, sink, cos, sin, wa, wb, lin_out, part_out, pieces, dense):
    kv = own[...] + rim[...].astype(F32)
    a, b = rotary(kv[:HALF], kv[HALF:HEAD_DIM], cos[...], -sin[...])
    high, low = split(sink[...])
    lin_out[:Q] = q[...]
    lin_out[Q : Q + HALF] = a.astype(BF)
    lin_out[Q + HALF : Q + HEAD_DIM] = b.astype(BF)
    lin_out[Q + HEAD_DIM : QKV] = kv[HEAD_DIM:].astype(BF)
    lin_out[QKV:] = jnp.concatenate([high, low], axis=0).astype(BF)
    lin = lin_out[:QKV]
    for k in range(8):
        pieces[idx[k]] = dot(wa[k], lin)
        pieces[idx[8 + k]] = dot(wb[k], lin)
    dense[WIDTH:] = jnp.zeros((WIDE - WIDTH, ROWS), F32)
    for k in range(DP):
        dense[k * CHUNK : (k + 1) * CHUNK] = pieces[k, :CHUNK]
    part_out[...] = dense[...].astype(BF).reshape(TN, COLS, ROWS)


def first_slice_kernel(at, got, residual, scale, out):
    total = got[0].astype(F32)
    for t in range(1, TN):
        total += got[t].astype(F32)
    mine = pl.ds(pl.multiple_of(at[0] * COLS, COLS), COLS)
    normed = residual[mine].astype(F32) * scale[...]
    high, low = split(jnp.sum(total * normed, axis=0, keepdims=True))
    for t in range(TN):
        out[t, :COLS] = total.astype(BF)
        out[t, COLS:] = rows_mask(16, high, low).astype(BF)


def mix_kernel(mixed, place, gains, out):
    mixture = dot(mixed[...].reshape(SLOTS, COLS), place[...], TNN).astype(BF)
    for t in range(TN):
        out[t, :COLS] = mixture
        out[t, COLS:] = gains[...]


def input_kernel(got, state, residual, scale, out):
    mean = jnp.zeros((1, ROWS), F32)
    for t in range(TN):
        mean += got[t, COLS : COLS + 1].astype(F32) + got[t, COLS + 1 : COLS + 2].astype(F32)
    mean = mean * (1.0 / WIDTH)
    for t in range(TN):
        n = COLS if t < TN - 1 else SPARE
        here = slice(t * COLS, t * COLS + n)
        normed = residual[here].astype(F32) * scale[...]
        out[here] = state[here] + scale[...] * (got[t, :n].astype(F32) - normed * mean)


def block_kernel(got, hidden, out, gain_out):
    gains = jnp.zeros((32, ROWS), F32)
    for t in range(TN):
        n = COLS if t < TN - 1 else SPARE
        here = slice(t * COLS, t * COLS + n)
        out[here] = hidden[here].astype(F32) + got[t, :n].astype(F32)
        gains += got[t, COLS:].astype(F32)
    gain_out[...] = gains


def qkv_weights_kernel(idx, chunk, la, lb, own, gain, out, bias_out, sink_out, gain_out):
    acc = jnp.zeros((CPAD, QKV), F32)
    bias = jnp.zeros((QKV, ROWS), F32)
    sinks = jnp.zeros((HEADS, ROWS), F32)
    for k in range(8):
        for j, ref in ((k, la), (8 + k, lb)):
            acc += dot(chunk[idx[j]], ref[k, :QKV], NT)
            bias += ref[k, :QKV].astype(F32)
            tail = ref[k, QKV:].astype(F32)
            sinks += tail[:HEADS] + tail[HEADS:]
    acc = acc[:CHUNK]
    out[...] = acc * gain[...]
    bias_out[...] = jnp.sum(bias, axis=1, keepdims=True)
    sink_out[...] = jnp.sum(sinks, axis=1, keepdims=True)
    gains = jnp.broadcast_to(jnp.sum(acc * own[...].astype(F32), axis=1, keepdims=True), (CHUNK, ROWS)).T[0:1]
    gains = jnp.concatenate([gains, jnp.zeros((1, 2 * ROWS - CHUNK), F32)], axis=1)
    high, low = split(gains)
    first, second = rows_mask(16, high, low)[:, :ROWS], rows_mask(16, high, low)[:, ROWS:]
    gain_out[...] = jnp.concatenate([first, second], axis=0).astype(BF)


def after(value, *first):
    return pl.pallas_call(
        lambda *refs: None,
        out_shape=shape(value.shape, value.dtype),
        in_specs=[ANY] * (1 + len(first)),
        out_specs=ANY,
        input_output_aliases={0: 0},
        name="after",
    )(held(value), *map(held, first))


def exchange(value, axis):
    return lax.all_to_all(value, axis, split_axis=0, concat_axis=0, tiled=True)


def spread(value, axis):
    return exchange(jnp.broadcast_to(value[None], (lax.axis_size(axis),) + value.shape), axis)


def copies(value, count):
    return jnp.broadcast_to(value[None], (count,) + value.shape)


def along_tensor(value, dz, dy):
    pairs = [(z * 4 + y, ((z + dz) % 2) * 4 + (y + dy) % 4) for z in range(2) for y in range(4)]
    return lax.ppermute(value, "tensor", pairs)


def along_dp(value, dx, dh, dc):
    pairs = [
        (x * 4 + h * 2 + c, ((x + dx) % 4) * 4 + ((h + dh) % 2) * 2 + (c + dc) % 2)
        for x in range(4)
        for h in range(2)
        for c in range(2)
    ]
    return lax.ppermute(value, "dp", pairs)


GATHER_FROM = ((0, 0), (0, 1), (3, 0), (1, 0), (2, 0), (3, 1), (1, 1), (2, 1))


def gather_dp(value, late):
    far = along_dp(value, 0, 1, 0)
    near = [along_dp(value, dx, 0, 0) for dx in (1, 3, 2)]
    more = [along_dp(far, dx, 0, 0) for dx in (1, 3, 2)]
    pieces = [value, far] + near + more
    this_core = call(stack_kernel, shape((8,) + value.shape, BF), pieces, us=2, after=late, name="stack")
    return this_core, along_dp(this_core, 0, 0, 1)


def gather_order(me):
    x, h, c = me // 4, (me // 2) % 2, me % 2
    return jnp.stack(
        [
            ((x + dx) % 4) * 4 + ((h + dh) % 2) * 2 + (c + dc) % 2
            for dc in range(2)
            for dx, dh in GATHER_FROM
        ]
    )


def gather_tensor(value, middle, early):
    n = COLS // 2
    x03 = along_tensor(value, 0, 1)
    x01 = along_tensor(value, 0, 3)
    x10 = along_tensor(value, 1, 0)

    if middle:
        x03, x01, x10 = (after(x, *middle) for x in (x03, x01, x10))
    up2 = along_tensor(jnp.stack([x03[:n], x10[:n]]), 0, 1)
    down2 = along_tensor(jnp.stack([x01[n:], x10[n:]]), 0, 3)
    side2 = along_tensor(jnp.stack([x03[n:], x01[:n]]), 1, 0)
    up3 = along_tensor(after(up2[1], early[0]), 0, 1)
    down3 = along_tensor(after(down2[1], early[-1]), 0, 3)
    return value, x03, x01, x10, up2, down2, side2, up3, down3


def tensor_order(me):
    z, y = me // 4, me % 4
    return jnp.stack([((z + r // 4) % 2) * 4 + (y + r % 4) % 4 for r in range(TN)])


def scatter_tensor(rows, steps=((), (), ())):
    n = COLS // 2

    def add(*values):
        total = values[0].astype(F32)
        for v in values[1:]:
            total = total + v.astype(F32)
        return total.astype(BF)

    sent = []

    def send(step, value, dz, dy):
        sent.append(after(value, *steps[step]) if steps[step] else value)
        return along_tensor(sent[-1], dz, dy)

    left = send(0, rows[6, :n], 0, 3)
    right = send(0, rows[6, n:], 0, 1)
    left2 = send(1, jnp.stack([add(rows[7, :n], left), rows[2, :n]]), 0, 3)
    right2 = send(1, jnp.stack([add(rows[5, n:], right), rows[2, n:]]), 0, 1)
    side2 = send(1, jnp.stack([rows[7, n:], rows[5, :n]]), 1, 0)
    join = jnp.concatenate
    left3 = send(2, add(rows[3], join([left2[1], side2[0]])), 0, 3)
    right3 = send(2, add(rows[1], join([side2[1], right2[1]])), 0, 1)
    side3 = send(2, add(rows[4], join([left2[0], right2[0]])), 1, 0)
    return (left3, right3, side3), sent[-3:]


def segments(lengths, token_index):
    seq_ends = jnp.cumsum(lengths)
    seq_starts = seq_ends - lengths
    segment = jnp.sum((token_index[:, None] >= seq_ends[None, :]).astype(jnp.int32), axis=1)
    member = segment[:, None] == jnp.arange(lengths.shape[0], dtype=jnp.int32)[None, :]
    position = token_index - jnp.sum(jnp.where(member, seq_starts[None, :], 0), axis=1)
    return (segment, position)


def pad_rows(a, rows):
    return jnp.pad(a, ((0, rows - a.shape[0]),) + ((0, 0),) * (a.ndim - 1))


def fold(chunks):
    return jnp.concatenate([chunks[:, 64 * i : 64 * i + 64] for i in range(3)], axis=2)


def unfold(rows):
    return jnp.concatenate([rows[:, :, 128 * i : 128 * i + 128] for i in range(3)], axis=1)


def local(
    residual,
    attn_gain,
    query_weight,
    query_bias,
    key_matrix,
    key_offset_bias,
    value_matrix,
    value_offset_bias,
    attention_sink_logits,
    out_weight,
    out_bias,
    mlp_gain,
    router_weight,
    router_bias,
    gate_weight,
    gate_bias,
    up_weight,
    up_bias,
    down_weight,
    down_bias,
    routes,
    lengths,
    cotangent,
):
    me_dp = lax.axis_index("dp")
    me_t = lax.axis_index("tensor")
    at = me_t[None].astype(jnp.int32)
    order_dp = gather_order(me_dp).astype(jnp.int32)
    order_t = tensor_order(me_t).astype(jnp.int32)

    gain_own = attn_gain.astype(F32)[:, None]
    own_qkv = jnp.concatenate([query_weight, key_matrix, value_matrix], axis=1)
    residual_t = residual.T
    inputs = residual_t.astype(F32)
    scale_one = lax.rsqrt(jnp.mean(inputs * inputs, axis=0, keepdims=True) + EPSILON)
    normed = (inputs * scale_one).astype(BF)
    normed_chunks = jnp.pad(normed.reshape(DP, CHUNK, ROWS), ((0, 0), (0, CPAD - CHUNK), (0, 0)))
    normed_rim = lax.ppermute(normed_chunks, "dp", [(i, i + 1) for i in range(DP - 1)])
    small = jnp.concatenate(
        [mlp_gain[:, None], out_bias[:, None], router_weight, jnp.zeros((CHUNK, 110), BF)], axis=1
    )
    out_all = lax.all_gather(pad_rows(jnp.concatenate([out_weight, small], axis=1), CPAD), "dp")
    qkv_a, qkv_b = gather_dp(pad_rows((own_qkv.astype(F32) * gain_own).astype(BF), CPAD), ())

    expert_ids = jnp.arange(EXPERTS, dtype=jnp.int32)
    member = jnp.any(routes.T[None, :, :] == expert_ids[:, None, None], axis=1)
    above = (jnp.arange(ROWS)[:, None] < jnp.arange(ROWS)[None, :]).astype(BF)
    rank = dot(member.astype(BF), above).astype(jnp.int32)
    place = (
        (rank[:, None, :] == jnp.arange(CAP, dtype=jnp.int32)[None, :, None]) & member[:, None, :]
    ).astype(BF).reshape(SLOTS, ROWS)
    member = member.astype(F32)

    cotangent_t = cotangent.T
    grad_ext = pad_rows(jnp.concatenate([cotangent_t, member.astype(BF)], axis=0), WIDE)
    grad_cols = lax.dynamic_slice_in_dim(grad_ext, me_t * COLS, COLS, 0)
    grad_slots = dot(place, grad_cols, NT).astype(BF).reshape(EXPERTS, CAP, COLS)
    grad_cols_t = call(
        turn_kernel, shape((COLS, SLOTS), BF), (exchange(grad_slots, "dp"),), us=2, name="turn_grad"
    )

    gate_t, up_t, down = gate_weight[0].T, up_weight[0].T, down_weight[0]
    gate_d, up_d, down_d = gate_weight[0], up_weight[0], jnp.pad(down.T, ((0, WIDE - WIDTH), (0, 0)))
    bias_on = (me_t == 0).astype(F32)[None]
    mine = (expert_ids == me_dp).astype(F32)[:, None]
    bias_router = router_bias.astype(F32)[:, None]

    starting_row = me_dp * ROWS
    token_index = starting_row + jnp.arange(ROWS, dtype=jnp.int32)
    segment, position = segments(lengths, token_index)
    key_index = starting_row - WINDOW + jnp.arange(ROWS + WINDOW, dtype=jnp.int32)
    key_segment, unused = segments(lengths, key_index)
    offset = token_index[None, :] - key_index[:, None]
    mask = (
        (segment[None, :] == key_segment[:, None])
        & (offset >= 0)
        & (offset < WINDOW)
        & (key_index[:, None] >= 0)
    ).astype(F32)
    frequency = ROPE_BASE ** (-2.0 * jnp.arange(HALF, dtype=F32) / HEAD_DIM)
    angle = position.astype(F32)[None, :] * frequency[:, None]
    cos, sin = jnp.cos(angle), jnp.sin(angle)
    unused, rim_position = segments(lengths, key_index[:WINDOW])
    rim_angle = rim_position.astype(F32)[None, :] * frequency[:, None]
    cos_rim, sin_rim = jnp.cos(rim_angle), jnp.sin(rim_angle)
    sink = jnp.repeat(attention_sink_logits.astype(F32), ROWS)[None]
    bias = jnp.concatenate([query_bias, key_offset_bias, value_offset_bias]).astype(F32)[None]
    ready = (mine, bias_router, mask, sink, grad_cols_t)
    query, own_kv, rim_kv = call(
        qkv_kernel,
        (shape((HEAD_DIM, CAT), BF), shape((2 * HEAD_DIM, ROWS), BF), shape((2 * HEAD_DIM, ROWS), BF)),
        (
            order_dp, qkv_a, qkv_b, normed_chunks, normed_rim, bias,
            cos, sin, cos_rim, sin_rim,
        ),
        smem=1,
        after=ready,
        mib=40, name="qkv",
    )
    probs, sink_probs, heads_out, branch, ext = call(
        attention_kernel,
        (
            shape((2 * WINDOW, CAT), F32),
            shape((1, CAT), F32),
            shape((Q, ROWS), BF),
            shape((WIDE, ROWS), BF),
            shape((WIDE, ROWS), F32),
        ),
        (query, rim_kv, own_kv, mask, sink, out_all),
        scratch=[pltpu.VMEM((WIDE, ROWS), F32)],
        mib=40, name="attention",
    )
    branch = exchange(branch.reshape(TN, COLS, ROWS), "tensor")

    grad_pieces = gather_tensor(after(grad_cols_t, qkv_a), (heads_out,), (heads_out,))
    tile = 256
    steps = SLOTS // tile
    def whole(a):
        return pl.BlockSpec(a.shape, lambda i, n=len(a.shape): (0,) * n)

    def lanes(a):
        n = len(a.shape)
        return pl.BlockSpec(a.shape[:-1] + (tile,), lambda i: (0,) * (n - 1) + (i,))

    back_outs = (shape((WIDE, SLOTS), BF), shape((FF + 8, SLOTS), F32), shape((EXPERTS, SLOTS), F32))
    grad_rows, down_back, chosen = pl.pallas_call(
        back_kernel,
        grid=(steps,),
        in_specs=[SMEM, SMEM] + [lanes(a) for a in grad_pieces] + [whole(down), whole(down_bias)],
        out_specs=[lanes(a) for a in back_outs],
        out_shape=back_outs,
        compiler_params=params(24),
        cost_estimate=cost(8),
        name="back",
    )(order_t, bias_on, *map(held, grad_pieces + (down, down_bias)))
    hidden_cols, out_rows = call(
        slice_kernel,
        (shape((TN, COLS, ROWS), BF), shape((EXPERTS, CAP, COLS), BF)),
        (at, branch, pad_rows(residual_t, WIDE), ext, place),
        smem=1,
        name="slice",
    )
    expert_cols = call(
        turn_kernel,
        shape((COLS, SLOTS), BF),
        (exchange(out_rows, "dp"),),
        after=(gate_d, up_d, down_d),
        us=2,
        name="turn",
    )
    router_t, router_d, inverse, gu_bias = call(
        tables_kernel,
        (
            shape((EXPERTS, WIDE), BF),
            shape((WIDE, EXPERTS), BF),
            shape((1, WIDE), F32),
            shape((2 * FF, 1), F32),
        ),
        (ext, gate_bias, up_bias),
        after=(expert_cols,),
        name="tables",
    )

    hidden = exchange(after(hidden_cols, expert_cols), "tensor").reshape(WIDE, ROWS)
    scale_two, gates = call(
        gates_kernel,
        (shape((1, ROWS), F32), shape((EXPERTS, ROWS), F32)),
        (hidden, ext, router_t, bias_router, member),
        name="gates",
    )
    pieces = gather_tensor(expert_cols, (), (gates, down_back))

    early = (grad_rows,)
    tiled = pieces + (chosen, down_back)
    full = (gate_t, up_t, gate_d, up_d, router_t, bias_router, gu_bias, inverse, mine)
    outs = (
        shape((TN, COLS, SLOTS), BF),
        shape((2 * FF, SLOTS), BF),
        shape((FF + 8, SLOTS), BF),
        shape((2 * FF, 1), F32),
    )
    rows_back, expert_grads, expert_hidden, bias_sums = pl.pallas_call(
        expert_kernel,
        grid=(steps,),
        in_specs=[SMEM] + [lanes(a) for a in tiled] + [whole(a) for a in full] + [ANY] * len(early),
        out_specs=[lanes(a) for a in outs[:3]] + [whole(outs[3])],
        out_shape=outs,
        scratch_shapes=[pltpu.VMEM((WIDE, tile), BF), pltpu.VMEM((WIDE, 1), F32), pltpu.VMEM((WIDE, tile), BF)],
        compiler_params=params(44),
        cost_estimate=cost(20),
        name="expert",
    )(order_t, *map(held, tiled + full + early))
    mixed_rows = pl.pallas_call(
        down_kernel,
        grid=(steps,),
        in_specs=[SMEM, lanes(outs[2]), whole(down_d), whole(down_bias)],
        out_specs=lanes(outs[0]),
        out_shape=outs[0],
        scratch_shapes=[pltpu.VMEM((WIDE, 1), F32), pltpu.VMEM((WIDE, tile), BF)],
        compiler_params=params(24),
        cost_estimate=cost(6),
        name="down",
    )(order_t, held(expert_hidden), held(down_d), held(down_bias * bias_on.astype(BF)))
    expert_in = pl.pallas_call(
        assemble_kernel,
        grid=(steps,),
        in_specs=[SMEM] + [lanes(a) for a in pieces] + [ANY],
        out_specs=pl.BlockSpec((WIDE, tile), lambda i: (0, i)),
        out_shape=shape((WIDE, SLOTS), BF),
        compiler_params=params(16),
        cost_estimate=cost(5),
        name="assemble",
    )(order_t, *map(held, pieces), held(expert_hidden))
    chunk_got = exchange(after(fold(normed_chunks), expert_hidden), "dp")
    first_chunk = unfold(chunk_got)

    (left, right, side), unused = scatter_tensor(rows_back, ((), (), (chunk_got,)))
    square = (COLS, SLOTS)

    def finish(rows, left, right, side, *early):
        return pl.pallas_call(
            finish_kernel,
            grid=(1,),
            in_specs=[SMEM, pl.BlockSpec((1,) + square, lambda i: (0, 0, 0))]
            + [pl.BlockSpec(square, lambda i: (0, 0))] * 3
            + [ANY] * 2,
            out_specs=pl.BlockSpec((SLOTS, COLS), lambda i: (0, 0)),
            out_shape=shape((SLOTS, COLS), BF),
            compiler_params=params(10),
            cost_estimate=cost(2),
            name="finish",
        )(at, *map(held, (rows, left, right, side) + early)).reshape(EXPERTS, CAP, COLS)

    back_cols = finish(rows_back, left, right, side, mixed_rows, mixed_rows)
    back_got = exchange(back_cols, "dp")
    back_tokens = call(
        combine_kernel, shape((TN, COLS, ROWS), BF), (at, back_got, place), smem=1,
        after=(expert_in,), name="combine",
    )
    back_all = exchange(back_tokens, "tensor").reshape(WIDE, ROWS)

    (mixed_left, mixed_right, mixed_side), mixed_sent = scatter_tensor(
        mixed_rows, ((left, right, side), (), (back_all,))
    )

    state, out_parts, q_grad, rim_grad, kv_grad, sink_grad = call(
        state_kernel,
        (
            shape((WIDTH, ROWS), F32),
            shape((DP, CPAD, Q + ROWS), BF),
            shape((Q, ROWS), BF),
            shape((2 * HEAD_DIM, WINDOW), BF),
            shape((2 * HEAD_DIM, ROWS), F32),
            shape((HEADS, ROWS), F32),
        ),
        (
            back_all, hidden, cotangent_t, ext, scale_two, gates, router_d, out_all, probs,
            sink_probs, query, rim_kv, own_kv, cos, sin, heads_out,
        ),
        scratch=[
            pltpu.VMEM((DP * CPAD, ROWS), F32),
            pltpu.VMEM((CPAD, ROWS), F32),
            pltpu.VMEM((WIDTH, ROWS), F32),
            pltpu.VMEM((DP, CPAD, ROWS), BF),
        ],
        mib=56, name="state",
    )
    rim_grad = lax.ppermute(rim_grad, "dp", [(i + 1, i) for i in range(DP - 1)])
    lin_grad, first_part = call(
        first_kernel,
        (shape((QKV + 16, ROWS), BF), shape((TN, COLS, ROWS), BF)),
        (order_dp, q_grad, kv_grad, rim_grad, sink_grad, cos, sin, qkv_a, qkv_b),
        smem=1,
        scratch=[pltpu.VMEM((DP, CPAD, ROWS), F32), pltpu.VMEM((WIDE, ROWS), F32)],
        after=tuple(mixed_sent),
        mib=40, name="first",
    )
    out_sums = lax.psum_scatter(out_parts, "dp", scatter_dimension=0)
    first_got = exchange(first_part, "tensor")

    def block(rows):
        return pl.BlockSpec((rows, COLS), lambda j: (0, j))

    grad_gate, grad_up = pl.pallas_call(
        gate_weights_kernel,
        grid=(TN,),
        in_specs=[
            pl.BlockSpec((2 * FF, SLOTS), lambda j: (0, 0)),
            pl.BlockSpec((COLS, SLOTS), lambda j: (j, 0)),
            ANY,
        ],
        out_specs=[block(FF), block(FF)],
        out_shape=(shape((FF, WIDTH), F32), shape((FF, WIDTH), F32)),
        compiler_params=params(16),
        cost_estimate=cost(12),
        name="gate_weights",
    )(held(expert_grads), held(expert_in), held(first_part))
    mixed_cols = finish(mixed_rows, mixed_left, mixed_right, mixed_side, back_all, grad_gate)
    first_cols = call(
        first_slice_kernel,
        shape((TN, COLS + 16, ROWS), BF),
        (at, first_got, pad_rows(residual_t, WIDE), scale_one),
        smem=1,
        name="first_slice",
    )
    lin_a, lin_b = gather_dp(after(lin_grad, first_cols, mixed_cols), ())
    grad_qkv, grad_bias, grad_sinks, gain_rows = call(
        qkv_weights_kernel,
        (shape((CHUNK, QKV), F32), shape((QKV, 1), F32), shape((HEADS, 1), F32), shape((32, ROWS), BF)),
        (order_dp, first_chunk, lin_a, lin_b, own_qkv, gain_own),
        smem=1,
        name="qkv_weights",
    )
    grad_down, grad_down_bias = pl.pallas_call(
        down_weights_kernel,
        grid=(TN,),
        in_specs=[
            pl.BlockSpec((FF + 8, SLOTS), lambda j: (0, 0)),
            pl.BlockSpec((COLS, SLOTS), lambda j: (j, 0)),
            ANY,
        ],
        out_specs=[block(FF), block(8)],
        out_shape=(shape((FF, WIDTH), F32), shape((8, WIDTH), F32)),
        compiler_params=params(16),
        cost_estimate=cost(9),
        name="down_weights",
    )(held(expert_hidden), held(grad_rows), held(first_got))

    first_all = exchange(first_cols, "tensor")
    mixed_got = exchange(after(mixed_cols, first_all), "dp")
    mixed_out = call(
        mix_kernel,
        shape((TN, COLS + 32, ROWS), BF),
        (mixed_got, place, gain_rows),
        after=(grad_down,),
        name="mix",
    )
    grad_input = call(
        input_kernel,
        shape((WIDTH, ROWS), F32),
        (first_all, state, residual_t, scale_one),
        name="input",
    )
    block_out, gains = call(
        block_kernel,
        (shape((WIDTH, ROWS), F32), shape((32, ROWS), F32)),
        (exchange(mixed_out, "tensor"), hidden),
        name="block",
    )
    gains = jnp.concatenate([gains[0] + gains[1], gains[16] + gains[17]])
    out_sums = out_sums[:CHUNK + 1].astype(F32)

    return (
        block_out.T,
        grad_input.T,
        gains[:CHUNK],
        grad_qkv[:, :Q],
        grad_bias[:Q, 0],
        grad_qkv[:, Q : Q + HEAD_DIM],
        grad_bias[Q : Q + HEAD_DIM, 0],
        grad_qkv[:, Q + HEAD_DIM :],
        grad_bias[Q + HEAD_DIM :, 0],
        grad_sinks[:, 0],
        out_sums[:CHUNK, :Q],
        out_sums[:CHUNK, Q + EXPERTS + 1],
        out_sums[:CHUNK, Q + EXPERTS],
        out_sums[:CHUNK, Q : Q + EXPERTS],
        out_sums[CHUNK, Q : Q + EXPERTS],
        grad_gate.T[None],
        bias_sums[None, :FF, 0],
        grad_up.T[None],
        bias_sums[None, FF:, 0],
        grad_down[None],
        grad_down_bias[:1],
    )


def solution(mesh):
    return jax.shard_map(
        local,
        mesh=mesh,
        in_specs=(
            P("dp", None),
            P("dp"),
            P("dp", "tensor"),
            P("tensor"),
            P("dp", "tensor"),
            P("tensor"),
            P("dp", "tensor"),
            P("tensor"),
            P("tensor"),
            P("dp", "tensor"),
            P("dp"),
            P("dp"),
            P("dp", None),
            P(),
            P("dp", None, "tensor"),
            P("dp", "tensor"),
            P("dp", None, "tensor"),
            P("dp", "tensor"),
            P("dp", "tensor", None),
            P("dp", None),
            P("dp", None),
            P(),
            P("dp", None),
        ),
        out_specs=(
            P("dp", None),
            P("dp", None),
            P("dp"),
            P("dp", "tensor"),
            P("tensor"),
            P("dp", "tensor"),
            P("tensor"),
            P("dp", "tensor"),
            P("tensor"),
            P("tensor"),
            P("dp", "tensor"),
            P("dp"),
            P("dp"),
            P("dp", None),
            P(),
            P("dp", None, "tensor"),
            P("dp", "tensor"),
            P("dp", None, "tensor"),
            P("dp", "tensor"),
            P("dp", "tensor", None),
            P("dp", None),
        ),
        check_vma=False,
    )
```
